32 devices in a mesh: groups: 2 (over y), wide: 4 (over z), narrow: 4 (over x, core).
Axes of the slice: x: 2, y: 2, z: 4, core: 2. Of those that a mesh axis runs over, the one named last changes fastest.
Arguments:
- tokens: bfloat16 [512, 4096], P(('groups', 'wide'), 'narrow'), parts along dimension 0, may hold values from -6 to 6
- routes: int32 [512, 8], P(('groups', 'wide')), parts along dimension 0, may hold values from 0 to 15, all different within a row; in each aligned block of 64 rows (0 to 63, 64 to 127, ...) at most 40 rows name the same one
- gate_weights: float32 [512, 8], P(('groups', 'wide')), parts along dimension 0, may hold values from 0.05 to 1
- delta_of: int32 [16], replicated, may hold values from 0 to 15, each once
- base_gate: bfloat16 [4096, 1536], P('wide', 'narrow'), may hold values from -0.09375 to 0.09375
- base_up: bfloat16 [4096, 1536], P('wide', 'narrow'), may hold values from -0.09375 to 0.09375
- base_down: bfloat16 [1536, 4096], P('wide', 'narrow'), may hold values from -0.15625 to 0.15625
- gate_left: bfloat16 [16, 4096, 32], P('wide', 'narrow'), may hold values from -0.09375 to 0.09375
- gate_right: bfloat16 [16, 32, 1536], P('wide', None, 'narrow'), may hold values from -0.5 to 0.5
- up_left: bfloat16 [16, 4096, 32], P('wide', 'narrow'), may hold values from -0.09375 to 0.09375
- up_right: bfloat16 [16, 32, 1536], P('wide', None, 'narrow'), may hold values from -0.5 to 0.5
- down_left: bfloat16 [16, 1536, 32], P('wide', 'narrow'), may hold values from -0.15625 to 0.15625
- down_right: bfloat16 [16, 32, 4096], P('wide', None, 'narrow'), may hold values from -0.5 to 0.5
Outputs:
- mixed_out: bfloat16 [512, 4096], P(('groups', 'wide'), 'narrow'), parts along dimension 0
The draws below stay inside these ranges and needn't reach their ends.
There are 2 independent parts, one for each index of `groups`. The reference program is written for one: setup_inputs(seed, part) draws one part's arguments, and reference() takes and returns one part's arrays. A program takes and returns all parts, laid end to end along the dimension named above; an argument that names none is the same for every part. Nothing has to cross between parts.
Inputs may be any that keep to these rules, and one draw needn't show every extreme that they name: `routes`: in each aligned block of 64 rows (the rows of one index of wide) no expert is named by more than 40 rows, and in some block some expert is named by exactly 40 rows.
All inputs are finite; a program needn't handle non-finite values.
Results may differ from the reference program's by a relative error of at most 0.0053.
Values may be sent and summed in bfloat16 or wider, within the bound.
No kernel may reach another device: no remote copies, remote signals or barrier semaphores. Data moves between devices by JAX's collectives and lax.ppermute only.
A program may use at most 64 MiB of HBM per device.

```python
import math
import jax
import jax.numpy as jnp
import numpy as np
from jax import lax

D = 4096
FF = 1536
R = 32
TOP = 8
BLK = 64
EXPERTS = 16
TOKENS = 256
CAP = 40


def steps_of(rng, extent, shards, least, high):
    gain, own = 1.0, jax.random.fold_in(rng, 6)
    for position, shards_of in shards:
        heights = jnp.exp(jax.random.uniform(jax.random.fold_in(own, position), (shards_of,), jnp.float32, least / len(shards), high / len(shards)))
        gain = gain * jnp.repeat(heights, extent[position] // shards_of).reshape([-1 if axis == position else 1 for axis in range(len(extent))])
    return gain


def deal_out(own_key, own, number, rows, count, top, bound, lean):
    order = jax.random.permutation(own_key, count)
    crowded, common = portions_of(count, rows * top, bound, lean, True), portions_of(count, rows * top, bound, lean, False)
    places = jnp.arange(count)

    def named(lengths, rotation):
        used = int((lengths > 0).sum())
        fixed = max(1, used // 4)
        moved = fixed + (places - fixed + rotation * (used - fixed)) % max(1, count - fixed)
        return jnp.zeros((count,), jnp.int32).at[order[jnp.where(places < fixed, places, moved)]].set(jnp.asarray(lengths, jnp.int32))

    lengths = jnp.where(number % 4 == 0, named(crowded, number // 4), named(common, number - number // 4 - 1))
    mixed = jax.random.permutation(jax.random.fold_in(own, 3), count)
    giver, sink = mixed[0:count // 2 * 2:2], mixed[1:count // 2 * 2:2]
    slack = jnp.minimum(lengths[giver] - 1, bound - lengths[sink]) // 2
    slack = jnp.where((giver == order[0]) | (sink == order[0]) | (lengths[sink] == 0), 0, jnp.maximum(slack, 0))
    moved = jax.random.randint(jax.random.fold_in(own, 4), (count // 2,), 0, 1 << 20) % (slack + 1)
    lengths = lengths.at[giver].add(-moved).at[sink].add(moved)
    items = jnp.searchsorted(jnp.cumsum(lengths), jnp.arange(rows * top), side="right").astype(jnp.int32)
    table = items.reshape(top, rows).T
    table = table[jax.random.permutation(jax.random.fold_in(own, 1), rows)]
    rotation = jax.random.randint(jax.random.fold_in(own, 2), (rows, 1), 0, top)
    return jnp.take_along_axis(table, (jnp.arange(top)[None, :] + rotation) % top, axis=1)


def portions_of(count, total, most, lean, full):
    portions = [(1 << 20) // math.isqrt(rank ** lean) + 1 for rank in range(1, count + 1)]
    largest = most if full else min(most, max(-(-total // count), total * portions[0] // sum(portions)))
    least = 1 if total - largest >= count - 1 else 0
    given, surplus = [largest] + [least] * (count - 1), total - largest - least * (count - 1)
    while surplus > 0:
        free = [i for i in range(1, count) if given[i] < largest] or [i for i in range(1, count) if given[i] < most]
        whole, remaining = sum([portions[i] for i in free]), surplus
        for i in free:
            more = min(most - given[i], max(1, remaining * portions[i] // whole), surplus)
            given[i] = given[i] + more
            surplus = surplus - more
    return np.array(given)


def gaussian(rng, dims, width, bound, split=(), kind=jnp.bfloat16):
    array = width * jax.random.normal(rng, dims, jnp.float32)
    if split:
        array = array * steps_of(rng, dims, split, -0.22, 0.18)
    return jnp.clip(array, -bound, bound).astype(kind)


def setup_inputs(seed: int = 0, part: int = 0) -> dict:
    arg_keys = jax.random.split(jax.random.key(seed), 14)
    part_splits = jax.random.split(jax.random.fold_in(arg_keys[13], part), 14)
    tokens = gaussian(part_splits[0], (TOKENS, D), 1.0, 6.0, ((0, 4), (1, 4)))
    routes_keys = jax.random.split(jax.random.fold_in(part_splits[1], 1), TOKENS // BLK)
    routes_turns = jax.random.permutation(jax.random.fold_in(part_splits[1], 3), TOKENS // BLK)
    routes = jax.vmap(lambda own, number: deal_out(jax.random.fold_in(part_splits[1], 2), own, number, BLK, EXPERTS, TOP, CAP, 2))(routes_keys, routes_turns).reshape((TOKENS, TOP))
    gate_weights = jnp.clip(0.05 + 0.95 * jax.random.uniform(part_splits[2], (TOKENS, TOP), jnp.float32) ** steps_of(part_splits[2], (TOKENS, TOP), ((0, 4),), -0.2, 0.2), 0.05, 1.0)
    delta_of = jax.random.permutation(arg_keys[3], EXPERTS).astype(jnp.int32)
    base_gate = gaussian(arg_keys[4], (D, FF), D ** -0.5, 0.09375, ((0, 4), (1, 4)))
    base_up = gaussian(arg_keys[5], (D, FF), D ** -0.5, 0.09375, ((0, 4), (1, 4)))
    base_down = gaussian(arg_keys[6], (FF, D), FF ** -0.5, 0.15625, ((0, 4), (1, 4)))
    gate_left = gaussian(arg_keys[7], (EXPERTS, D, R), D ** -0.5, 0.09375, ((0, 4), (1, 4)))
    gate_right = gaussian(arg_keys[8], (EXPERTS, R, FF), (4 * R) ** -0.5, 0.5, ((0, 4), (2, 4)))
    up_left = gaussian(arg_keys[9], (EXPERTS, D, R), D ** -0.5, 0.09375, ((0, 4), (1, 4)))
    up_right = gaussian(arg_keys[10], (EXPERTS, R, FF), (4 * R) ** -0.5, 0.5, ((0, 4), (2, 4)))
    down_left = gaussian(arg_keys[11], (EXPERTS, FF, R), FF ** -0.5, 0.15625, ((0, 4), (1, 4)))
    down_right = gaussian(arg_keys[12], (EXPERTS, R, D), (4 * R) ** -0.5, 0.5, ((0, 4), (2, 4)))
    return {"tokens": tokens, "routes": routes, "gate_weights": gate_weights, "delta_of": delta_of, "base_gate": base_gate, "base_up": base_up, "base_down": base_down, "gate_left": gate_left, "gate_right": gate_right, "up_left": up_left, "up_right": up_right, "down_left": down_left, "down_right": down_right}


def rebuild(base, left, right):
    return (base.astype(jnp.float32) + jnp.dot(left, right, preferred_element_type=jnp.float32)).astype(jnp.bfloat16)


def reference(tokens, routes, gate_weights, delta_of, base_gate, base_up, base_down, gate_left, gate_right, up_left, up_right, down_left, down_right):
    token_count = tokens.shape[0]
    experts = delta_of.shape[0]
    expert_ids = jnp.arange(experts, dtype=jnp.int32)
    onehot = (routes[:, :, None] == expert_ids[None, None, :]).astype(jnp.int32)
    routed = jnp.sum(onehot, axis=1)
    blocked = routed.reshape(token_count // BLK, BLK, experts)
    before = (jnp.cumsum(blocked, axis=1) - blocked).reshape(token_count, experts)
    place_in = jnp.sum(onehot * before[:, None, :], axis=2).astype(jnp.int32)
    block_of = (jnp.arange(token_count, dtype=jnp.int32) // BLK)[:, None]
    slot_count = (token_count // BLK) * CAP
    flat_index = (routes * slot_count + block_of * CAP + place_in).reshape(-1).astype(jnp.int32)
    token_ids = jnp.repeat(jnp.arange(token_count, dtype=jnp.int32), routes.shape[1])
    source = jnp.full((experts * slot_count,), token_count, jnp.int32).at[flat_index].set(token_ids).reshape(experts, slot_count)
    scales = jnp.zeros((experts * slot_count,), jnp.float32).at[flat_index].set(gate_weights.reshape(-1).astype(jnp.float32)).reshape(experts, slot_count)
    padded = jnp.concatenate([tokens, jnp.zeros((1, tokens.shape[1]), tokens.dtype)], axis=0)

    def visit(running, inputs):
        expert, row_ids, row_scales = inputs
        delta_id = delta_of[expert]
        w_gate = rebuild(base_gate, gate_left[delta_id], gate_right[delta_id])
        w_up = rebuild(base_up, up_left[delta_id], up_right[delta_id])
        w_down = rebuild(base_down, down_left[delta_id], down_right[delta_id])
        rows_in = padded[row_ids]
        gate_act = jnp.dot(rows_in, w_gate, preferred_element_type=jnp.float32)
        up_act = jnp.dot(rows_in, w_up, preferred_element_type=jnp.float32)
        hidden = (jax.nn.silu(gate_act) * up_act).astype(jnp.bfloat16)
        result = jnp.dot(hidden, w_down, preferred_element_type=jnp.float32).astype(jnp.bfloat16)
        running = running.at[row_ids].add(row_scales[:, None] * result.astype(jnp.float32))
        return running, None

    start_sum = jnp.zeros((token_count + 1, tokens.shape[1]), jnp.float32)
    running, unused = lax.scan(visit, start_sum, (expert_ids, source, scales))
    return running[:token_count].astype(jnp.bfloat16)
```

```python
import functools

import jax
import jax.numpy as jnp
from jax import lax
from jax.experimental import pallas as pl
from jax.experimental.pallas import tpu as pltpu
from jax.sharding import PartitionSpec as P

F32 = jnp.float32
BF16 = jnp.bfloat16


def with_zero_row(rows):
    return jnp.concatenate([rows, jnp.zeros((1, rows.shape[1]), rows.dtype)], axis=0)


def rebuild(base_rows, left_rows, right_factor):
    product = jnp.einsum(
        "ecr,erf->ecf", left_rows, right_factor, preferred_element_type=jnp.float32
    )
    return (base_rows.astype(jnp.float32)[None] + product).astype(jnp.bfloat16)


def gathered_shards(
    tokens,
    routes,
    gate_weights,
    delta_of,
    base_gate,
    base_up,
    base_down,
    gate_left,
    gate_right,
    up_left,
    up_right,
    down_left,
    down_right,
):
    block_rows, top_count = routes.shape
    feature_part = tokens.shape[1]
    exp_here = gate_left.shape[0]
    wide_count = lax.axis_size("wide")
    experts = wide_count * exp_here
    capacity = max(2, block_rows * top_count * 5 // (4 * experts))
    slot_total = experts * capacity
    expert_ids = lax.broadcasted_iota(jnp.int32, (1, 1, experts), 2)
    onehot = (routes[:, :, None] == expert_ids).astype(jnp.float32)
    routed = jnp.sum(onehot, axis=1)
    row_index = lax.broadcasted_iota(jnp.int32, (block_rows, block_rows), 0)
    col_index = lax.broadcasted_iota(jnp.int32, (block_rows, block_rows), 1)
    earlier_mask = (col_index < row_index).astype(jnp.float32)
    before = jnp.dot(
        earlier_mask, routed, preferred_element_type=jnp.float32, precision=lax.Precision.HIGHEST
    )
    place_in = jnp.sum(onehot * before[:, None, :], axis=2).astype(jnp.int32)
    delta_ids = jnp.sum(onehot * delta_of.astype(jnp.float32)[None, None, :], axis=2).astype(
        jnp.int32
    )
    position = delta_ids * capacity + place_in
    every_row = lax.all_gather(tokens, "wide", axis=0, tiled=True)
    every_place = lax.all_gather(position, "wide", axis=0, tiled=True)
    own_first = lax.axis_index("wide") * (exp_here * capacity)
    local_place = every_place - own_first
    owned = (local_place >= 0) & (local_place < exp_here * capacity)
    block_ids = lax.broadcasted_iota(jnp.int32, every_place.shape, 0) // block_rows
    target = jnp.where(owned, block_ids * (exp_here * capacity) + local_place, slot_total)
    every_token = lax.broadcasted_iota(jnp.int32, every_place.shape, 0)
    picked_rows = (
        jnp.full((slot_total,), every_row.shape[0], jnp.int32)
        .at[target.reshape(-1)]
        .set(every_token.reshape(-1), mode="drop")
    )
    local_rows = jnp.take(with_zero_row(every_row), picked_rows, axis=0).reshape(
        wide_count, exp_here, capacity, feature_part
    )
    slot_rows = lax.all_gather(local_rows, "narrow", axis=3, tiled=True)
    left_gate, left_up, left_down = (
        lax.all_gather(gate_left, "narrow", axis=1, tiled=True),
        lax.all_gather(up_left, "narrow", axis=1, tiled=True),
        lax.all_gather(down_left, "narrow", axis=1, tiled=True),
    )
    base_rows_gate = lax.all_gather(base_gate, "wide", axis=0, tiled=True)
    base_rows_up = lax.all_gather(base_up, "wide", axis=0, tiled=True)
    columns = slot_rows
    dense_gate = rebuild(base_rows_gate, left_gate, gate_right)
    dense_up = rebuild(base_rows_up, left_up, up_right)
    gate_sum = jnp.einsum("secd,edf->secf", columns, dense_gate, preferred_element_type=jnp.float32)
    up_sum = jnp.einsum("secd,edf->secf", columns, dense_up, preferred_element_type=jnp.float32)
    hidden = (jax.nn.silu(gate_sum) * up_sum).astype(jnp.bfloat16)
    hidden_all = lax.all_gather(hidden, "narrow", axis=3, tiled=True)
    dense_down = rebuild(
        lax.all_gather(base_down, "wide", axis=0, tiled=True), left_down, down_right
    )
    columns = hidden_all
    expert_out = jnp.einsum(
        "secf,efd->secd", columns, dense_down, preferred_element_type=jnp.float32
    ).astype(jnp.bfloat16)
    returned = lax.all_to_all(expert_out, "wide", split_axis=0, concat_axis=0, tiled=True).reshape(
        slot_total, feature_part
    )
    picked = jnp.take(returned, position.reshape(-1), axis=0).reshape(
        block_rows, top_count, feature_part
    )
    mixed_out = jnp.sum(gate_weights[:, :, None] * picked.astype(jnp.float32), axis=1)
    return mixed_out.astype(jnp.bfloat16)


def dot_rows(a, b):
    return lax.dot_general(a, b, (((1,), (1,)), ((), ())), preferred_element_type=F32)


def left_kernel(count, *refs):
    xs, (lg, lu), outs = refs[:count], refs[count : count + 2], refs[count + 2 :]
    cols = lg.shape[0]
    for x, out in zip(xs, outs):
        out[:, :cols] = dot_rows(x[...], lg[...]).astype(BF16)
        out[:, cols:] = dot_rows(x[...], lu[...]).astype(BF16)


def base_kernel(count, place, x, wg, wu, *refs):
    outs, total = refs[:count], refs[count]
    cols = wg.shape[1]
    total[:, :cols] = jnp.dot(x[...], wg[...], preferred_element_type=F32)
    total[:, cols:] = jnp.dot(x[...], wu[...], preferred_element_type=F32)
    rows = outs[0].shape[0]
    for k in range(count):
        start = pl.multiple_of(lax.rem(place[0] + k, count) * rows, rows)
        outs[k][...] = total[pl.ds(start, rows), :].astype(BF16)


def hidden_kernel(count, held, *refs):
    gs, (pls, weight), rs = refs[:count], refs[count : count + 2], refs[count + 2 : 2 * count + 2]
    hsum, hl, *_ = refs[2 * count + 2 :]
    rows, both = gs[0].shape
    cols = both // 2
    rank_cols = rs[0].shape[1]
    rank = rank_cols // held
    base = sum(g[...].astype(F32) for g in gs)
    gate, up = base[:, :cols], base[:, cols:]
    low = sum(pls[pl.ds(n * rows, rows), :].astype(F32) for n in range(pls.shape[0] // rows)).astype(BF16)
    owner = lax.broadcasted_iota(jnp.int32, (rows, rank_cols), 1) // rank
    acc = jnp.zeros((rows, cols), F32)
    for k in range(count):
        here = low[:, k * 2 * rank_cols : (k + 1) * 2 * rank_cols]
        low_gate, low_up = here[:, :rank_cols], here[:, rank_cols:]
        zero = jnp.zeros_like(low_gate)
        lhs_gate = jnp.concatenate([jnp.where(owner == i, low_gate, zero) for i in range(held)], axis=0)
        lhs_up = jnp.concatenate([jnp.where(owner == i, low_up, zero) for i in range(held)], axis=0)
        g = jnp.dot(lhs_gate, rs[k][0], preferred_element_type=F32)
        u = jnp.dot(lhs_up, rs[k][1], preferred_element_type=F32)
        parts = []
        for i in range(held):
            gi = gate + g[i * rows : (i + 1) * rows]
            ui = up + u[i * rows : (i + 1) * rows]
            h = (gi / (1.0 + jnp.exp(-gi))) * ui
            slot = k * held + i
            hw = h * weight[:, slot : slot + 1]
            acc += hw
            parts.append(hw.astype(BF16))
        back = dot_rows(jnp.concatenate(parts, axis=0), rs[k][2])
        block = jnp.zeros((rows, rank_cols), F32)
        for i in range(held):
            block += jnp.where(owner == i, back[i * rows : (i + 1) * rows], 0.0)
        hl[k] = block.astype(BF16)
    hsum[...] = acc.astype(BF16)


def down_kernel(count, place, hs, w, rd, *refs):
    outs, total = refs[:count], refs[count]
    rows = outs[0].shape[0]
    inner = w.shape[0]
    rank_cols = rd.shape[0]
    low = sum(hs[pl.ds(n * rows, rows), inner:].astype(F32) for n in range(hs.shape[0] // rows)).astype(BF16)
    total[...] = jnp.dot(hs[:, :inner], w[...], preferred_element_type=F32)
    low_rows = jnp.concatenate(
        [low[:, j * rank_cols : (j + 1) * rank_cols] for j in ((count - k) % count for k in range(count))], axis=0
    )
    added = jnp.dot(low_rows, rd[...], preferred_element_type=F32)
    for k in range(count):
        start = pl.multiple_of(lax.rem(place[0] + k, count) * rows, rows)
        outs[k][...] = (total[pl.ds(start, rows), :] + added[k * rows : (k + 1) * rows]).astype(BF16)


VMEM = pl.BlockSpec(memory_space=pltpu.VMEM)
SMEM = pl.BlockSpec(memory_space=pltpu.SMEM)
PARAMS = pltpu.CompilerParams(vmem_limit_bytes=24 * 2**20)


def along(axis, count, step):
    return lambda a: lax.ppermute(a, axis, [(i, (i + step) % count) for i in range(count)])


def stationary_shards(
    tokens,
    routes,
    gate_weights,
    delta_of,
    base_gate,
    base_up,
    base_down,
    gate_left,
    gate_right,
    up_left,
    up_right,
    down_left,
    down_right,
):
    count = lax.axis_size("wide")
    rows, top_count = routes.shape
    held, rank = gate_left.shape[0], gate_left.shape[2]
    experts = held * count
    rank_cols = held * rank
    inner = base_gate.shape[1]
    features = base_down.shape[1]
    place = lax.axis_index("wide")
    place_arr = place[None].astype(jnp.int32)

    def swap(a):
        return lax.ppermute(
            a, ("wide", "narrow"), [(i * count + j, j * count + i) for i in range(count) for j in range(count)]
        )

    def spread(parts, sign):
        return [parts[0]] + [along("wide", count, sign * k)(parts[k]) for k in range(1, count)]

    own_features = lax.all_gather(swap(tokens), "narrow", axis=0, tiled=True)
    blocks = spread([tokens] * count, 1)

    packed = jnp.stack(
        [
            gate_right.reshape(rank_cols, inner),
            up_right.reshape(rank_cols, inner),
            jnp.swapaxes(down_left, 1, 2).reshape(rank_cols, inner),
        ]
    )
    factors = spread([packed] * count, -1)

    expert_ids = lax.broadcasted_iota(jnp.int32, (1, 1, experts), 2)
    named = routes[:, :, None] == expert_ids
    delta_ids = jnp.sum(jnp.where(named, delta_of[None, None, :], 0), axis=2)
    slots = lax.rem(delta_ids - place * held + experts, experts)
    weight = jnp.sum(jnp.where(slots[:, :, None] == expert_ids, gate_weights[:, :, None], 0.0), axis=1)

    left_t = [jnp.swapaxes(a, 1, 2).reshape(rank_cols, a.shape[1]) for a in (gate_left, up_left)]
    low = pl.pallas_call(
        functools.partial(left_kernel, count),
        out_shape=[jax.ShapeDtypeStruct((rows, 2 * rank_cols), BF16)] * count,
        in_specs=[VMEM] * (count + 2),
        out_specs=[VMEM] * count,
        compiler_params=PARAMS,
    )(*blocks, *left_t)
    low = jnp.concatenate(spread(low, -1), axis=1)
    low = lax.all_gather(low, "narrow", axis=0, tiled=True)

    sums = pl.pallas_call(
        functools.partial(base_kernel, count),
        out_shape=[jax.ShapeDtypeStruct((rows, 2 * inner), BF16)] * count,
        in_specs=[SMEM] + [VMEM] * 3,
        out_specs=[VMEM] * count,
        scratch_shapes=[pltpu.VMEM((count * rows, 2 * inner), F32)],
        compiler_params=PARAMS,
    )(place_arr, own_features, base_gate, base_up)
    sums = spread(sums, 1)

    hsum, hl = pl.pallas_call(
        functools.partial(hidden_kernel, count, held),
        out_shape=[
            jax.ShapeDtypeStruct((rows, inner), BF16),
            jax.ShapeDtypeStruct((count, rows, rank_cols), BF16),
        ],
        in_specs=[VMEM] * (2 * count + 2),
        out_specs=[VMEM] * 2,
        compiler_params=PARAMS,
    )(*sums, low, weight, *factors)

    hs = jnp.concatenate([swap(hsum)] + spread([hl[k] for k in range(count)], 1), axis=1)
    hs = lax.all_gather(hs, "narrow", axis=0, tiled=True)
    outs = pl.pallas_call(
        functools.partial(down_kernel, count),
        out_shape=[jax.ShapeDtypeStruct((rows, features), BF16)] * count,
        in_specs=[SMEM] + [VMEM] * 3,
        out_specs=[VMEM] * count,
        scratch_shapes=[pltpu.VMEM((count * rows, features), F32)],
        compiler_params=PARAMS,
    )(place_arr, hs, base_down, down_right.reshape(rank_cols, features))
    outs = spread(outs, 1)
    return sum(o.astype(F32) for o in outs).astype(BF16)


def solution(mesh):
    square = mesh.shape["wide"] == mesh.shape["narrow"]
    return jax.shard_map(
        stationary_shards if square else gathered_shards,
        mesh=mesh,
        in_specs=(
            P(("groups", "wide"), "narrow"),
            P(("groups", "wide"), None),
            P(("groups", "wide"), None),
            P(),
            P("wide", "narrow"),
            P("wide", "narrow"),
            P("wide", "narrow"),
            P("wide", "narrow", None),
            P("wide", None, "narrow"),
            P("wide", "narrow", None),
            P("wide", None, "narrow"),
            P("wide", "narrow", None),
            P("wide", None, "narrow"),
        ),
        out_specs=P(("groups", "wide"), "narrow"),
        check_vma=False,
    )
```

```python
import functools
import math

import jax
import jax.numpy as jnp
from jax import lax
from jax.experimental import pallas as pl
from jax.experimental.pallas import tpu as pltpu
from jax.sharding import PartitionSpec as P

F32 = jnp.float32
BF16 = jnp.bfloat16


def with_zero_row(rows):
    return jnp.concatenate([rows, jnp.zeros((1, rows.shape[1]), rows.dtype)], axis=0)


def rebuild(base_rows, left_rows, right_factor):
    product = jnp.einsum(
        "ecr,erf->ecf", left_rows, right_factor, preferred_element_type=jnp.float32
    )
    return (base_rows.astype(jnp.float32)[None] + product).astype(jnp.bfloat16)


def gathered_shards(
    tokens,
    routes,
    gate_weights,
    delta_of,
    base_gate,
    base_up,
    base_down,
    gate_left,
    gate_right,
    up_left,
    up_right,
    down_left,
    down_right,
):
    block_rows, top_count = routes.shape
    feature_part = tokens.shape[1]
    exp_here = gate_left.shape[0]
    wide_count = lax.axis_size("wide")
    experts = wide_count * exp_here
    capacity = max(2, block_rows * top_count * 5 // (4 * experts))
    slot_total = experts * capacity
    expert_ids = lax.broadcasted_iota(jnp.int32, (1, 1, experts), 2)
    onehot = (routes[:, :, None] == expert_ids).astype(jnp.float32)
    routed = jnp.sum(onehot, axis=1)
    row_index = lax.broadcasted_iota(jnp.int32, (block_rows, block_rows), 0)
    col_index = lax.broadcasted_iota(jnp.int32, (block_rows, block_rows), 1)
    earlier_mask = (col_index < row_index).astype(jnp.float32)
    before = jnp.dot(
        earlier_mask, routed, preferred_element_type=jnp.float32, precision=lax.Precision.HIGHEST
    )
    place_in = jnp.sum(onehot * before[:, None, :], axis=2).astype(jnp.int32)
    delta_ids = jnp.sum(onehot * delta_of.astype(jnp.float32)[None, None, :], axis=2).astype(
        jnp.int32
    )
    position = delta_ids * capacity + place_in
    every_row = lax.all_gather(tokens, "wide", axis=0, tiled=True)
    every_place = lax.all_gather(position, "wide", axis=0, tiled=True)
    own_first = lax.axis_index("wide") * (exp_here * capacity)
    local_place = every_place - own_first
    owned = (local_place >= 0) & (local_place < exp_here * capacity)
    block_ids = lax.broadcasted_iota(jnp.int32, every_place.shape, 0) // block_rows
    target = jnp.where(owned, block_ids * (exp_here * capacity) + local_place, slot_total)
    every_token = lax.broadcasted_iota(jnp.int32, every_place.shape, 0)
    picked_rows = (
        jnp.full((slot_total,), every_row.shape[0], jnp.int32)
        .at[target.reshape(-1)]
        .set(every_token.reshape(-1), mode="drop")
    )
    local_rows = jnp.take(with_zero_row(every_row), picked_rows, axis=0).reshape(
        wide_count, exp_here, capacity, feature_part
    )
    slot_rows = lax.all_gather(local_rows, "narrow", axis=3, tiled=True)
    left_gate, left_up, left_down = (
        lax.all_gather(gate_left, "narrow", axis=1, tiled=True),
        lax.all_gather(up_left, "narrow", axis=1, tiled=True),
        lax.all_gather(down_left, "narrow", axis=1, tiled=True),
    )
    base_rows_gate = lax.all_gather(base_gate, "wide", axis=0, tiled=True)
    base_rows_up = lax.all_gather(base_up, "wide", axis=0, tiled=True)
    columns = slot_rows
    dense_gate = rebuild(base_rows_gate, left_gate, gate_right)
    dense_up = rebuild(base_rows_up, left_up, up_right)
    gate_sum = jnp.einsum("secd,edf->secf", columns, dense_gate, preferred_element_type=jnp.float32)
    up_sum = jnp.einsum("secd,edf->secf", columns, dense_up, preferred_element_type=jnp.float32)
    hidden = (jax.nn.silu(gate_sum) * up_sum).astype(jnp.bfloat16)
    hidden_all = lax.all_gather(hidden, "narrow", axis=3, tiled=True)
    dense_down = rebuild(
        lax.all_gather(base_down, "wide", axis=0, tiled=True), left_down, down_right
    )
    columns = hidden_all
    expert_out = jnp.einsum(
        "secf,efd->secd", columns, dense_down, preferred_element_type=jnp.float32
    ).astype(jnp.bfloat16)
    returned = lax.all_to_all(expert_out, "wide", split_axis=0, concat_axis=0, tiled=True).reshape(
        slot_total, feature_part
    )
    picked = jnp.take(returned, position.reshape(-1), axis=0).reshape(
        block_rows, top_count, feature_part
    )
    mixed_out = jnp.sum(gate_weights[:, :, None] * picked.astype(jnp.float32), axis=1)
    return mixed_out.astype(jnp.bfloat16)


def dot_rows(a, b):
    return lax.dot_general(a, b, (((1,), (1,)), ((), ())), preferred_element_type=F32)


def left_kernel(count, side, place, *refs):
    xs, ls, outs, held = refs[:count], refs[count : count + side], refs[count + side : -1], refs[-1]
    for m in range(count):
        held[m] = xs[m][...]
    for q in range(side):
        total = jnp.zeros(outs[q].shape, F32)
        for e in range(side):
            total += dot_rows(held[place[0] ^ place[1] ^ (side * q + e)], ls[e][...])
        outs[q][...] = total.astype(BF16)


def base_kernel(count, side, place, *refs):
    xs, (wg, wu), outs, total = refs[:side], refs[side : side + 2], refs[side + 2 : -1], refs[-1]
    cols = wg.shape[1]
    rows = outs[0].shape[0]
    x = jnp.concatenate([x[...] for x in xs], axis=0)
    total[:, :cols] = jnp.dot(x, wg[...], preferred_element_type=F32)
    total[:, cols:] = jnp.dot(x, wu[...], preferred_element_type=F32)
    for k in range(count):
        turn = lax.rem(place[0] ^ place[1] ^ k, side)
        start = pl.multiple_of((turn * side + k // side) * rows, rows)
        outs[k][...] = total[pl.ds(start, rows), :].astype(outs[k].dtype)


def hidden_kernel(count, held, place, *refs):
    gs, (low, weight), rs = refs[:count], refs[count : count + 2], refs[count + 2 : 2 * count + 2]
    outs, hl = refs[2 * count + 2 : 3 * count + 2], refs[3 * count + 2]
    rows, both = gs[0].shape
    cols = both // 2
    rank_cols = rs[0].shape[1]
    rank = rank_cols // held
    base = sum(g[...].astype(F32) for g in gs)
    gate, up = base[:, :cols], base[:, cols:]
    owner = lax.broadcasted_iota(jnp.int32, (rows, rank_cols), 1) // rank
    acc = jnp.zeros((rows, cols), F32)
    for k in range(count):
        start = pl.multiple_of((place[0] ^ k) * rows, rows)
        here = low[pl.ds(start, rows), :]
        low_gate, low_up = here[:, :rank_cols], here[:, rank_cols:]
        zero = jnp.zeros_like(low_gate)
        lhs_gate = jnp.concatenate([jnp.where(owner == i, low_gate, zero) for i in range(held)], axis=0)
        lhs_up = jnp.concatenate([jnp.where(owner == i, low_up, zero) for i in range(held)], axis=0)
        g = jnp.dot(lhs_gate, rs[k][0], preferred_element_type=F32)
        u = jnp.dot(lhs_up, rs[k][1], preferred_element_type=F32)
        parts = []
        for i in range(held):
            gi = gate + g[i * rows : (i + 1) * rows]
            ui = up + u[i * rows : (i + 1) * rows]
            h = (gi / (1.0 + jnp.exp(-gi))) * ui
            slot = k * held + i
            hw = h * weight[:, slot : slot + 1]
            acc += hw
            parts.append(hw.astype(BF16))
        back = dot_rows(jnp.concatenate(parts, axis=0), rs[k][2])
        block = jnp.zeros((rows, rank_cols), F32)
        for i in range(held):
            block += jnp.where(owner == i, back[i * rows : (i + 1) * rows], 0.0)
        hl[place[0] ^ place[1] ^ k] = block.astype(BF16)
    outs[0][:, :cols] = acc.astype(BF16)
    outs[0][:, cols:] = hl[0]
    for m in range(1, count):
        outs[m][...] = hl[m]


def down_kernel(count, place, hs, w, rd, *refs):
    outs, total = refs[:count], refs[count]
    rows = outs[0].shape[0]
    inner = w.shape[0]
    total[...] = jnp.dot(hs[:, :inner], w[...], preferred_element_type=F32)
    total[...] += jnp.dot(hs[:, inner:], rd[...], preferred_element_type=F32)
    for k in range(count):
        start = pl.multiple_of(lax.rem(place[0] + k, count) * rows, rows)
        outs[k][...] = total[pl.ds(start, rows), :].astype(outs[k].dtype)


VMEM = pl.BlockSpec(memory_space=pltpu.VMEM)
ANY = pl.BlockSpec(memory_space=pl.ANY)
SMEM = pl.BlockSpec(memory_space=pltpu.SMEM)
PARAMS = pltpu.CompilerParams(vmem_limit_bytes=24 * 2**20)


def stationary_shards(
    tokens,
    routes,
    gate_weights,
    delta_of,
    base_gate,
    base_up,
    base_down,
    gate_left,
    gate_right,
    up_left,
    up_right,
    down_left,
    down_right,
):
    count = lax.axis_size("wide")
    rows = tokens.shape[0]
    held, rank = gate_left.shape[0], gate_left.shape[2]
    experts = held * count
    rank_cols = held * rank
    inner = base_gate.shape[1]
    features = base_down.shape[1]
    place = lax.axis_index("wide")
    spot = lax.axis_index("narrow")
    places = jnp.stack([place, spot]).astype(jnp.int32)
    side = math.isqrt(count)
    steps = range(1, count)

    def swap(a, k=0):
        pairs = [(i * count + j, (j ^ k) * count + i) for i in range(count) for j in range(count)]
        return lax.ppermute(a, ("wide", "narrow"), pairs)

    def across(a, axis, k):
        return lax.ppermute(a, axis, [(i, i ^ k) for i in range(count)])

    def ahead(a, k):
        return lax.ppermute(a, "wide", [(i, (i + k) % count) for i in range(count)])

    def after(a, other):
        return lax.optimization_barrier((a, other))[0]

    def doubled(a, axis, order, other):
        blocks = {0: a}
        for bit in order:
            for k, b in list(blocks.items()):
                blocks[k ^ bit] = across(after(b, other) if k else b, axis, bit)
        return [blocks[k] for k in range(count)]

    bits = [1 << b for b in range(count.bit_length() - 1)]

    spread = []
    for m in range(count):
        pairs = [
            (w * count + j, (m ^ (w // side * side + j % side)) * count + j // side * side + w % side)
            for w in range(count)
            for j in range(count)
        ]
        spread.append(lax.ppermute(tokens, ("wide", "narrow"), pairs))

    mine = [spread[side * a] for a in range(side)]
    holds = spot // side == place // side
    for a in range(side):
        come = 0
        for b in range(1, side):
            pairs = [
                (z * count + n, z * count + (n ^ (side * b)))
                for z in range(count)
                for n in range(count)
                if z // side == n // side
            ]
            come += lax.ppermute(spread[side * a], ("wide", "narrow"), pairs)
        mine[a] = jnp.where(holds, mine[a], come)
    mine = jnp.concatenate(mine, axis=0)
    own_features = [mine] + [across(mine, "narrow", e) for e in range(1, side)]

    left = jnp.concatenate(
        [jnp.swapaxes(a, 1, 2).reshape(rank_cols, a.shape[1]) for a in (gate_left, up_left)], axis=0
    )
    left = [left] + [across(left, "narrow", e) for e in range(1, side)]

    low = pl.pallas_call(
        functools.partial(left_kernel, count, side),
        out_shape=[jax.ShapeDtypeStruct((rows, 2 * rank_cols), BF16)] * side,
        in_specs=[SMEM] + [VMEM] * (count + side),
        out_specs=[VMEM] * side,
        scratch_shapes=[pltpu.VMEM((count, *tokens.shape), BF16)],
        compiler_params=PARAMS,
    )(places, *spread, *left)
    low = sum(swap(low[q], side * q).astype(F32) for q in range(side)).astype(BF16)

    sums = pl.pallas_call(
        functools.partial(base_kernel, count, side),
        out_shape=[jax.ShapeDtypeStruct((rows, 2 * inner), F32 if k == 0 else BF16) for k in range(count)],
        in_specs=[SMEM] + [VMEM] * (side + 2),
        out_specs=[VMEM] * count,
        scratch_shapes=[pltpu.VMEM((count * rows, 2 * inner), F32)],
        compiler_params=PARAMS,
    )(places, *own_features, base_gate, base_up)

    packed = jnp.stack(
        [
            gate_right.reshape(rank_cols, inner),
            up_right.reshape(rank_cols, inner),
            jnp.swapaxes(down_left, 1, 2).reshape(rank_cols, inner),
        ]
    )
    factors = doubled(packed, "wide", bits[::-1], sums[0])
    low = lax.all_gather(after(low, sums[0]), "narrow", axis=0, tiled=True)
    sums = [sums[0]] + [across(sums[k], "wide", k) for k in steps]

    expert_ids = lax.broadcasted_iota(jnp.int32, (1, 1, experts), 2)
    named = routes[:, :, None] == expert_ids
    delta_ids = jnp.sum(jnp.where(named, delta_of[None, None, :], 0), axis=2)
    slots = ((delta_ids // held) ^ place) * held + delta_ids % held
    weight = jnp.sum(jnp.where(slots[:, :, None] == expert_ids, gate_weights[:, :, None], 0.0), axis=1)

    hidden = pl.pallas_call(
        functools.partial(hidden_kernel, count, held),
        out_shape=[
            jax.ShapeDtypeStruct((rows, rank_cols + (inner if k == 0 else 0)), BF16) for k in range(count)
        ],
        in_specs=[SMEM] + [VMEM] * (2 * count + 2),
        out_specs=[VMEM] * count,
        scratch_shapes=[pltpu.VMEM((count, rows, rank_cols), BF16)],
        compiler_params=PARAMS,
    )(places, *sums, low, weight, *factors)

    hidden = [swap(hidden[k], k) for k in range(count)]
    low_sum = sum(h[:, -rank_cols:].astype(F32) for h in hidden).astype(BF16)
    hs = jnp.concatenate([hidden[0][:, :inner], low_sum], axis=1)
    hs = lax.all_gather(hs, "narrow", axis=0, tiled=True)
    outs = pl.pallas_call(
        functools.partial(down_kernel, count),
        out_shape=[jax.ShapeDtypeStruct((rows, features), F32 if k == 0 else BF16) for k in range(count)],
        in_specs=[SMEM] + [VMEM] * 3,
        out_specs=[VMEM] * count,
        scratch_shapes=[pltpu.VMEM((count * rows, features), F32)],
        compiler_params=PARAMS,
    )(places, hs, base_down, down_right.reshape(rank_cols, features))
    return sum([outs[0]] + [ahead(outs[k], k).astype(F32) for k in steps]).astype(BF16)


def solution(mesh):
    count = mesh.shape["wide"]
    square = count == mesh.shape["narrow"] == math.isqrt(count) ** 2 and count & (count - 1) == 0
    return jax.shard_map(
        stationary_shards if square else gathered_shards,
        mesh=mesh,
        in_specs=(
            P(("groups", "wide"), "narrow"),
            P(("groups", "wide"), None),
            P(("groups", "wide"), None),
            P(),
            P("wide", "narrow"),
            P("wide", "narrow"),
            P("wide", "narrow"),
            P("wide", "narrow", None),
            P("wide", None, "narrow"),
            P("wide", "narrow", None),
            P("wide", None, "narrow"),
            P("wide", "narrow", None),
            P("wide", None, "narrow"),
        ),
        out_specs=P(("groups", "wide"), "narrow"),
        check_vma=False,
    )
```

```python
import functools
import math

import jax
import jax.numpy as jnp
from jax import lax
from jax.experimental import pallas as pl
from jax.experimental.pallas import tpu as pltpu
from jax.sharding import PartitionSpec as P

F32 = jnp.float32
BF16 = jnp.bfloat16


def with_zero_row(rows):
    return jnp.concatenate([rows, jnp.zeros((1, rows.shape[1]), rows.dtype)], axis=0)


def rebuild(base_rows, left_rows, right_factor):
    product = jnp.einsum(
        "ecr,erf->ecf", left_rows, right_factor, preferred_element_type=jnp.float32
    )
    return (base_rows.astype(jnp.float32)[None] + product).astype(jnp.bfloat16)


def gathered_shards(
    tokens,
    routes,
    gate_weights,
    delta_of,
    base_gate,
    base_up,
    base_down,
    gate_left,
    gate_right,
    up_left,
    up_right,
    down_left,
    down_right,
):
    block_rows, top_count = routes.shape
    feature_part = tokens.shape[1]
    exp_here = gate_left.shape[0]
    wide_count = lax.axis_size("wide")
    experts = wide_count * exp_here
    capacity = max(2, block_rows * top_count * 5 // (4 * experts))
    slot_total = experts * capacity
    expert_ids = lax.broadcasted_iota(jnp.int32, (1, 1, experts), 2)
    onehot = (routes[:, :, None] == expert_ids).astype(jnp.float32)
    routed = jnp.sum(onehot, axis=1)
    row_index = lax.broadcasted_iota(jnp.int32, (block_rows, block_rows), 0)
    col_index = lax.broadcasted_iota(jnp.int32, (block_rows, block_rows), 1)
    earlier_mask = (col_index < row_index).astype(jnp.float32)
    before = jnp.dot(
        earlier_mask, routed, preferred_element_type=jnp.float32, precision=lax.Precision.HIGHEST
    )
    place_in = jnp.sum(onehot * before[:, None, :], axis=2).astype(jnp.int32)
    delta_ids = jnp.sum(onehot * delta_of.astype(jnp.float32)[None, None, :], axis=2).astype(
        jnp.int32
    )
    position = delta_ids * capacity + place_in
    every_row = lax.all_gather(tokens, "wide", axis=0, tiled=True)
    every_place = lax.all_gather(position, "wide", axis=0, tiled=True)
    own_first = lax.axis_index("wide") * (exp_here * capacity)
    local_place = every_place - own_first
    owned = (local_place >= 0) & (local_place < exp_here * capacity)
    block_ids = lax.broadcasted_iota(jnp.int32, every_place.shape, 0) // block_rows
    target = jnp.where(owned, block_ids * (exp_here * capacity) + local_place, slot_total)
    every_token = lax.broadcasted_iota(jnp.int32, every_place.shape, 0)
    picked_rows = (
        jnp.full((slot_total,), every_row.shape[0], jnp.int32)
        .at[target.reshape(-1)]
        .set(every_token.reshape(-1), mode="drop")
    )
    local_rows = jnp.take(with_zero_row(every_row), picked_rows, axis=0).reshape(
        wide_count, exp_here, capacity, feature_part
    )
    slot_rows = lax.all_gather(local_rows, "narrow", axis=3, tiled=True)
    left_gate, left_up, left_down = (
        lax.all_gather(gate_left, "narrow", axis=1, tiled=True),
        lax.all_gather(up_left, "narrow", axis=1, tiled=True),
        lax.all_gather(down_left, "narrow", axis=1, tiled=True),
    )
    base_rows_gate = lax.all_gather(base_gate, "wide", axis=0, tiled=True)
    base_rows_up = lax.all_gather(base_up, "wide", axis=0, tiled=True)
    columns = slot_rows
    dense_gate = rebuild(base_rows_gate, left_gate, gate_right)
    dense_up = rebuild(base_rows_up, left_up, up_right)
    gate_sum = jnp.einsum("secd,edf->secf", columns, dense_gate, preferred_element_type=jnp.float32)
    up_sum = jnp.einsum("secd,edf->secf", columns, dense_up, preferred_element_type=jnp.float32)
    hidden = (jax.nn.silu(gate_sum) * up_sum).astype(jnp.bfloat16)
    hidden_all = lax.all_gather(hidden, "narrow", axis=3, tiled=True)
    dense_down = rebuild(
        lax.all_gather(base_down, "wide", axis=0, tiled=True), left_down, down_right
    )
    columns = hidden_all
    expert_out = jnp.einsum(
        "secf,efd->secd", columns, dense_down, preferred_element_type=jnp.float32
    ).astype(jnp.bfloat16)
    returned = lax.all_to_all(expert_out, "wide", split_axis=0, concat_axis=0, tiled=True).reshape(
        slot_total, feature_part
    )
    picked = jnp.take(returned, position.reshape(-1), axis=0).reshape(
        block_rows, top_count, feature_part
    )
    mixed_out = jnp.sum(gate_weights[:, :, None] * picked.astype(jnp.float32), axis=1)
    return mixed_out.astype(jnp.bfloat16)


def dot_rows(a, b):
    return lax.dot_general(a, b, (((1,), (1,)), ((), ())), preferred_element_type=F32)


def left_kernel(count, side, place, *refs):
    xs, ls, outs, held = refs[:count], refs[count : count + side], refs[count + side : -1], refs[-1]
    for m in range(count):
        held[m] = xs[m][...]
    rows = outs[0].shape[0]
    total = jnp.zeros((side * rows, outs[0].shape[1]), F32)
    for e in range(side):
        x = jnp.concatenate([held[place[0] ^ place[1] ^ (side * q + e)] for q in range(side)], axis=0)
        total += dot_rows(x, ls[e][...])
    for q in range(side):
        outs[q][...] = total[q * rows : (q + 1) * rows].astype(BF16)


def base_kernel(count, side, place, *refs):
    xs, (wg, wu), outs, total = refs[:side], refs[side : side + 2], refs[side + 2 : -1], refs[-1]
    cols = wg.shape[1]
    rows = outs[0].shape[0]
    x = jnp.concatenate([x[...] for x in xs], axis=0)
    total[:, :cols] = jnp.dot(x, wg[...], preferred_element_type=F32)
    total[:, cols:] = jnp.dot(x, wu[...], preferred_element_type=F32)
    for k in range(count):
        turn = lax.rem(place[0] ^ place[1] ^ k, side)
        start = pl.multiple_of((turn * side + k // side) * rows, rows)
        outs[k][...] = total[pl.ds(start, rows), :].astype(outs[k].dtype)


def hidden_kernel(count, held, place, *refs):
    gs, (low, weight), rs = refs[:count], refs[count : count + 2], refs[count + 2 : 2 * count + 2]
    hsum, *outs, hl = refs[2 * count + 2 :]
    side = len(outs)
    rows, both = gs[0].shape
    cols = both // 2
    rank_cols = rs[0].shape[1]
    rank = rank_cols // held
    base = sum(g[...].astype(F32) for g in gs)
    gate, up = base[:, :cols], base[:, cols:]
    owner = lax.broadcasted_iota(jnp.int32, (rows, rank_cols), 1) // rank
    acc = jnp.zeros((rows, cols), F32)
    for k in range(count):
        start = pl.multiple_of((place[0] ^ k) * rows, rows)
        here = low[pl.ds(start, rows), :]
        low_gate, low_up = here[:, :rank_cols], here[:, rank_cols:]
        zero = jnp.zeros_like(low_gate)
        lhs_gate = jnp.concatenate([jnp.where(owner == i, low_gate, zero) for i in range(held)], axis=0)
        lhs_up = jnp.concatenate([jnp.where(owner == i, low_up, zero) for i in range(held)], axis=0)
        g = jnp.dot(lhs_gate, rs[k][0], preferred_element_type=F32)
        u = jnp.dot(lhs_up, rs[k][1], preferred_element_type=F32)
        parts = []
        for i in range(held):
            gi = gate + g[i * rows : (i + 1) * rows]
            ui = up + u[i * rows : (i + 1) * rows]
            h = (0.5 * gi) * (1.0 + jnp.tanh(0.5 * gi)) * ui
            slot = k * held + i
            hw = h * weight[:, slot : slot + 1]
            acc += hw
            parts.append(hw.astype(BF16))
        back = dot_rows(jnp.concatenate(parts, axis=0), rs[k][2])
        block = jnp.zeros((rows, rank_cols), F32)
        for i in range(held):
            block += jnp.where(owner == i, back[i * rows : (i + 1) * rows], 0.0)
        hl[place[0] ^ place[1] ^ k] = block
    hsum[...] = acc.astype(BF16)
    for e in range(side):
        for b in range(side):
            outs[e][:, b * rank_cols : (b + 1) * rank_cols] = hl[side * b + e].astype(outs[e].dtype)


def down_kernel(count, place, hs, w, rd, *refs):
    outs, total = refs[:count], refs[count]
    rows = outs[0].shape[0]
    inner = w.shape[0]
    total[...] = jnp.dot(hs[:, :inner], w[...], preferred_element_type=F32)
    total[...] += jnp.dot(hs[:, inner:], rd[...], preferred_element_type=F32)
    for k in range(count):
        start = pl.multiple_of(lax.rem(place[0] + k, count) * rows, rows)
        outs[k][...] = total[pl.ds(start, rows), :].astype(outs[k].dtype)


VMEM = pl.BlockSpec(memory_space=pltpu.VMEM)
ANY = pl.BlockSpec(memory_space=pl.ANY)
SMEM = pl.BlockSpec(memory_space=pltpu.SMEM)
PARAMS = pltpu.CompilerParams(vmem_limit_bytes=24 * 2**20)

SEP, YR = True, False
TIES = {'C': ['sums0'], 'lowag': ['sums0'], 'far': ['X1', 'X3', 'xe2'], 'mc': ['sent']}

def stationary_shards(tokens, routes, gate_weights, delta_of, base_gate, base_up, base_down, gate_left, gate_right, up_left, up_right, down_left, down_right):
    count = lax.axis_size("wide")
    rows = tokens.shape[0]
    held, rank = gate_left.shape[0], gate_left.shape[2]
    experts = held * count
    rank_cols = held * rank
    inner = base_gate.shape[1]
    features = base_down.shape[1]
    place = lax.axis_index("wide")
    spot = lax.axis_index("narrow")
    places = jnp.stack([place, spot, lax.axis_index("groups")]).astype(jnp.int32)
    side = math.isqrt(count)
    steps = range(1, count)
    memo, busy = {}, set()

    def get(name):
        if name not in memo:
            assert name not in busy, "cycle"
            busy.add(name)
            memo[name] = nodes[name]()
        return memo[name]

    def tied(a, name):
        deps = [get(d) for d in TIES.get(name, ())]
        return lax.optimization_barrier((a, deps))[0] if deps else a

    def swap(a, k=0):
        pairs = [(i * count + j, (j ^ k) * count + i) for i in range(count) for j in range(count)]
        return lax.ppermute(a, ("wide", "narrow"), pairs)

    def across(a, axis, k):
        return lax.ppermute(a, axis, [(i, i ^ k) for i in range(count)])

    def ahead(a, k):
        return lax.ppermute(a, "wide", [(i, (i + k) % count) for i in range(count)])

    nodes = {}

    def node(f):
        nodes[f.__name__] = f
        return f

    def X(m):
        pairs = [
            (w * count + j, (m ^ (w // side * side + j % side)) * count + j // side * side + w % side)
            for w in range(count)
            for j in range(count)
        ]
        return lax.ppermute(tied(tokens, f"X{m}"), ("wide", "narrow"), pairs)
    for m in range(count):
        nodes[f"X{m}"] = functools.partial(X, m)

    def xe(m):
        pairs = [
            (z * count + n, z * count + (n ^ side))
            for z in range(count)
            for n in range(count)
            if z // side == n // side
        ]
        return lax.ppermute(tied(get(f"X{m}"), f"xe{m}"), ("wide", "narrow"), pairs)
    nodes["xe0"] = lambda: xe(0)
    nodes["xe2"] = lambda: xe(2)

    @node
    def mine():
        holds = spot // side == place // side
        return jnp.concatenate([jnp.where(holds, get(f"X{m}"), get(f"xe{m}")) for m in (0, 2)], axis=0)

    @node
    def mc():
        return across(tied(get("mine"), "mc"), "narrow", 1)

    @node
    def Lp():
        return jnp.concatenate(
            [jnp.swapaxes(a, 1, 2).reshape(rank_cols, a.shape[1]) for a in (gate_left, up_left)], axis=0
        )

    @node
    def Lc():
        return across(tied(get("Lp"), "Lc"), "narrow", 1)

    @node
    def PL():
        spread = [get(f"X{m}") for m in range(count)]
        left = [tied(get("Lp"), "PL"), get("Lc")]
        if SEP:
            return pl.pallas_call(
                functools.partial(left_kernel, count, side),
                out_shape=[jax.ShapeDtypeStruct((rows, 2 * rank_cols), BF16)] * side,
                in_specs=[SMEM] + [VMEM] * (count + side),
                out_specs=[VMEM] * side,
                scratch_shapes=[pltpu.VMEM((count, *tokens.shape), BF16)],
                compiler_params=PARAMS,
            )(places, *spread, *left)
        return pl.pallas_call(
            functools.partial(left_kernel, count, side),
            out_shape=[jax.ShapeDtypeStruct((side * rows, 2 * rank_cols), kind) for kind in (F32, BF16)],
            in_specs=[SMEM] + [VMEM] * (count + side),
            out_specs=[VMEM] * 2,
            scratch_shapes=[pltpu.VMEM((count, *tokens.shape), BF16)],
            compiler_params=PARAMS,
        )(places, *spread, *left)

    @node
    def sent():
        return get("PL")[1]

    @node
    def PLt0():
        return swap(tied(get("PL")[0], "PLt0"), 0)

    @node
    def PLt1():
        return swap(tied(get("PL")[1], "PLt1"), side)

    @node
    def PLx():
        return across(tied(get("PL")[1], "PLx"), "narrow", side)

    @node
    def low():
        if SEP:
            return (get("PLt0").astype(F32) + get("PLt1").astype(F32)).astype(BF16)
        return (get("PL")[0] + get("PLx").astype(F32)).astype(BF16)

    @node
    def PLc():
        return across(tied(get("low"), "PLc"), "narrow", 1)

    @node
    def lowag():
        return lax.all_gather(tied(get("low"), "lowag"), "narrow", axis=0, tiled=True)

    @node
    def Rp():
        return jnp.stack(
            [
                gate_right.reshape(rank_cols, inner),
                up_right.reshape(rank_cols, inner),
                jnp.swapaxes(down_left, 1, 2).reshape(rank_cols, inner),
            ]
        )

    @node
    def part():
        if not YR:
            return get("Rp")
        half = rank_cols // 2
        return lax.dynamic_slice_in_dim(get("Rp"), lax.axis_index("groups") * half, half, axis=1)

    @node
    def far():
        return across(tied(get("part"), "far"), "wide", 2)

    @node
    def near():
        return across(tied(get("part"), "near"), "wide", 1)

    @node
    def C():
        return across(tied(get("far"), "C"), "wide", 1)

    @node
    def close():
        return across(jnp.stack([get("part"), tied(get("far"), "close")]), "wide", 1)

    @node
    def brought():
        return jnp.stack([get("close")[0], get("far"), get("close")[1]])

    @node
    def Y():
        return lax.ppermute(tied(get("brought"), "Y"), "groups", [(0, 1), (1, 0)])

    @node
    def mm1():
        own = [tied(get("mine"), "mm1"), get("mc")]
        if SEP:
            return pl.pallas_call(
                functools.partial(base_kernel, count, side),
                out_shape=[jax.ShapeDtypeStruct((rows, 2 * inner), F32 if k == 0 else BF16) for k in range(count)],
                in_specs=[SMEM] + [VMEM] * (side + 2),
                out_specs=[VMEM] * count,
                scratch_shapes=[pltpu.VMEM((count * rows, 2 * inner), F32)],
                compiler_params=PARAMS,
            )(places, *own, base_gate, base_up)
        wide_cols = 2 * inner + 2 * rank_cols
        return pl.pallas_call(
            functools.partial(base_kernel, count, side),
            out_shape=[jax.ShapeDtypeStruct((rows, wide_cols), F32 if k == 0 else BF16) for k in range(count)],
            in_specs=[SMEM] + [VMEM] * (2 * side + 2),
            out_specs=[VMEM] * count,
            scratch_shapes=[
                pltpu.VMEM((count * rows, 2 * inner), F32),
                pltpu.VMEM((count * rows, 2 * rank_cols), BF16),
            ],
            compiler_params=PARAMS,
        )(places, *own, get("low"), get("PLc"), base_gate, base_up)

    @node
    def sums0():
        return get("mm1")[0]

    for k in range(1, count):
        nodes[f"P{k}"] = lambda k=k: across(tied(get("mm1")[k], f"P{k}"), "wide", k)

    @node
    def weight():
        expert_ids = lax.broadcasted_iota(jnp.int32, (1, 1, experts), 2)
        named = routes[:, :, None] == expert_ids
        delta_ids = jnp.sum(jnp.where(named, delta_of[None, None, :], 0), axis=2)
        slots = ((delta_ids // held) ^ place) * held + delta_ids % held
        return jnp.sum(jnp.where(slots[:, :, None] == expert_ids, gate_weights[:, :, None], 0.0), axis=1)

    sums = [get("sums0")] + [get(f"P{k}") for k in steps]
    extra = [get("lowag")] if SEP else []
    if YR:
        fac = [get("Rp"), get("brought"), get("Y")]
        more = [pltpu.VMEM((count - 1, *get("Rp").shape), BF16)]
    else:
        fac = [get("Rp"), get("near"), get("far"), get("C")]
        more = []
    ins = [places, *sums, *extra, get("weight"), *fac]
    hsum, *parts = pl.pallas_call(
        functools.partial(hidden_kernel, count, held),
        out_shape=[jax.ShapeDtypeStruct((rows, inner), BF16)]
        + [jax.ShapeDtypeStruct((rows, side * rank_cols), F32 if e == 0 else BF16) for e in range(side)],
        in_specs=[SMEM] + [VMEM] * (len(ins) - 1),
        out_specs=[VMEM] * (side + 1),
        scratch_shapes=[pltpu.VMEM((count, rows, rank_cols), F32)] + more,
        compiler_params=PARAMS,
    )(*ins)
    part = parts[0] + sum(across(parts[e], "narrow", e).astype(F32) for e in range(1, side))
    part = jnp.split(part.astype(BF16), side, axis=1)
    first = swap(jnp.concatenate([hsum, part[0]], axis=1))
    low_sum = first[:, inner:].astype(F32) + sum(swap(part[b], side * b).astype(F32) for b in range(1, side))
    hs = jnp.concatenate([first[:, :inner], low_sum.astype(BF16)], axis=1)
    hs = lax.all_gather(hs, "narrow", axis=0, tiled=True)
    outs = pl.pallas_call(
        functools.partial(down_kernel, count),
        out_shape=[jax.ShapeDtypeStruct((rows, features), F32 if k == 0 else BF16) for k in range(count)],
        in_specs=[SMEM] + [VMEM] * 3,
        out_specs=[VMEM] * count,
        scratch_shapes=[pltpu.VMEM((count * rows, features), F32)],
        compiler_params=PARAMS,
    )(places, hs, base_down, down_right.reshape(rank_cols, features))
    return sum([outs[0]] + [ahead(outs[k], k).astype(F32) for k in steps]).astype(BF16)


def solution(mesh):
    count = mesh.shape["wide"]
    square = count == mesh.shape["narrow"] == math.isqrt(count) ** 2 and count & (count - 1) == 0
    return jax.shard_map(
        stationary_shards if square else gathered_shards,
        mesh=mesh,
        in_specs=(
            P(("groups", "wide"), "narrow"),
            P(("groups", "wide"), None),
            P(("groups", "wide"), None),
            P(),
            P("wide", "narrow"),
            P("wide", "narrow"),
            P("wide", "narrow"),
            P("wide", "narrow", None),
            P("wide", None, "narrow"),
            P("wide", "narrow", None),
            P("wide", None, "narrow"),
            P("wide", "narrow", None),
            P("wide", None, "narrow"),
        ),
        out_specs=P(("groups", "wide"), "narrow"),
        check_vma=False,
    )
```

```python
import functools
import math

import jax
import jax.numpy as jnp
from jax import lax
from jax.experimental import pallas as pl
from jax.experimental.pallas import tpu as pltpu
from jax.sharding import PartitionSpec as P

F32 = jnp.float32
BF16 = jnp.bfloat16


def with_zero_row(rows):
    return jnp.concatenate([rows, jnp.zeros((1, rows.shape[1]), rows.dtype)], axis=0)


def rebuild(base_rows, left_rows, right_factor):
    product = jnp.einsum(
        "ecr,erf->ecf", left_rows, right_factor, preferred_element_type=jnp.float32
    )
    return (base_rows.astype(jnp.float32)[None] + product).astype(jnp.bfloat16)


def gathered_shards(
    tokens,
    routes,
    gate_weights,
    delta_of,
    base_gate,
    base_up,
    base_down,
    gate_left,
    gate_right,
    up_left,
    up_right,
    down_left,
    down_right,
):
    block_rows, top_count = routes.shape
    feature_part = tokens.shape[1]
    exp_here = gate_left.shape[0]
    wide_count = lax.axis_size("wide")
    experts = wide_count * exp_here
    capacity = max(2, block_rows * top_count * 5 // (4 * experts))
    slot_total = experts * capacity
    expert_ids = lax.broadcasted_iota(jnp.int32, (1, 1, experts), 2)
    onehot = (routes[:, :, None] == expert_ids).astype(jnp.float32)
    routed = jnp.sum(onehot, axis=1)
    row_index = lax.broadcasted_iota(jnp.int32, (block_rows, block_rows), 0)
    col_index = lax.broadcasted_iota(jnp.int32, (block_rows, block_rows), 1)
    earlier_mask = (col_index < row_index).astype(jnp.float32)
    before = jnp.dot(
        earlier_mask, routed, preferred_element_type=jnp.float32, precision=lax.Precision.HIGHEST
    )
    place_in = jnp.sum(onehot * before[:, None, :], axis=2).astype(jnp.int32)
    delta_ids = jnp.sum(onehot * delta_of.astype(jnp.float32)[None, None, :], axis=2).astype(
        jnp.int32
    )
    position = delta_ids * capacity + place_in
    every_row = lax.all_gather(tokens, "wide", axis=0, tiled=True)
    every_place = lax.all_gather(position, "wide", axis=0, tiled=True)
    own_first = lax.axis_index("wide") * (exp_here * capacity)
    local_place = every_place - own_first
    owned = (local_place >= 0) & (local_place < exp_here * capacity)
    block_ids = lax.broadcasted_iota(jnp.int32, every_place.shape, 0) // block_rows
    target = jnp.where(owned, block_ids * (exp_here * capacity) + local_place, slot_total)
    every_token = lax.broadcasted_iota(jnp.int32, every_place.shape, 0)
    picked_rows = (
        jnp.full((slot_total,), every_row.shape[0], jnp.int32)
        .at[target.reshape(-1)]
        .set(every_token.reshape(-1), mode="drop")
    )
    local_rows = jnp.take(with_zero_row(every_row), picked_rows, axis=0).reshape(
        wide_count, exp_here, capacity, feature_part
    )
    slot_rows = lax.all_gather(local_rows, "narrow", axis=3, tiled=True)
    left_gate, left_up, left_down = (
        lax.all_gather(gate_left, "narrow", axis=1, tiled=True),
        lax.all_gather(up_left, "narrow", axis=1, tiled=True),
        lax.all_gather(down_left, "narrow", axis=1, tiled=True),
    )
    base_rows_gate = lax.all_gather(base_gate, "wide", axis=0, tiled=True)
    base_rows_up = lax.all_gather(base_up, "wide", axis=0, tiled=True)
    columns = slot_rows
    dense_gate = rebuild(base_rows_gate, left_gate, gate_right)
    dense_up = rebuild(base_rows_up, left_up, up_right)
    gate_sum = jnp.einsum("secd,edf->secf", columns, dense_gate, preferred_element_type=jnp.float32)
    up_sum = jnp.einsum("secd,edf->secf", columns, dense_up, preferred_element_type=jnp.float32)
    hidden = (jax.nn.silu(gate_sum) * up_sum).astype(jnp.bfloat16)
    hidden_all = lax.all_gather(hidden, "narrow", axis=3, tiled=True)
    dense_down = rebuild(
        lax.all_gather(base_down, "wide", axis=0, tiled=True), left_down, down_right
    )
    columns = hidden_all
    expert_out = jnp.einsum(
        "secf,efd->secd", columns, dense_down, preferred_element_type=jnp.float32
    ).astype(jnp.bfloat16)
    returned = lax.all_to_all(expert_out, "wide", split_axis=0, concat_axis=0, tiled=True).reshape(
        slot_total, feature_part
    )
    picked = jnp.take(returned, position.reshape(-1), axis=0).reshape(
        block_rows, top_count, feature_part
    )
    mixed_out = jnp.sum(gate_weights[:, :, None] * picked.astype(jnp.float32), axis=1)
    return mixed_out.astype(jnp.bfloat16)


def dot_rows(a, b):
    return lax.dot_general(a, b, (((1,), (1,)), ((), ())), preferred_element_type=F32)


def left_kernel(count, side, place, *refs):
    xs, ls, outs, held = refs[:count], refs[count : count + side], refs[count + side : -1], refs[-1]
    for m in range(count):
        held[m] = xs[m][...]
    rows = outs[0].shape[0]
    total = jnp.zeros((side * rows, outs[0].shape[1]), F32)
    for e in range(side):
        x = jnp.concatenate([held[place[0] ^ place[1] ^ (side * q + e)] for q in range(side)], axis=0)
        total += dot_rows(x, ls[e][...])
    for q in range(side):
        outs[q][...] = total[q * rows : (q + 1) * rows].astype(BF16)


def base_kernel(count, side, place, *refs):
    xs, (wg, wu), outs, total = refs[:side], refs[side : side + 2], refs[side + 2 : -1], refs[-1]
    cols = wg.shape[1]
    rows = outs[0].shape[0]
    x = jnp.concatenate([x[...] for x in xs], axis=0)
    total[:, :cols] = jnp.dot(x, wg[...], preferred_element_type=F32)
    total[:, cols:] = jnp.dot(x, wu[...], preferred_element_type=F32)
    for k in range(count):
        turn = lax.rem(place[0] ^ place[1] ^ k, side)
        start = pl.multiple_of((turn * side + k // side) * rows, rows)
        outs[k][...] = total[pl.ds(start, rows), :].astype(outs[k].dtype)


def expert_terms(k, spot, held, place, gate, up, low, weight, factors):
    rows, cols = gate.shape
    rank_cols = factors.shape[1]
    owner = lax.broadcasted_iota(jnp.int32, (rows, rank_cols), 1) // (rank_cols // held)
    here = low[pl.ds(pl.multiple_of((place[0] ^ k) * rows, rows), rows), :]
    sides = []
    for half in (here[:, :rank_cols], here[:, rank_cols:]):
        zero = jnp.zeros_like(half)
        sides.append(jnp.concatenate([jnp.where(owner == i, half, zero) for i in range(held)], axis=0))
    g = jnp.dot(sides[0], factors[0], preferred_element_type=F32)
    u = jnp.dot(sides[1], factors[1], preferred_element_type=F32)
    total, parts = jnp.zeros((rows, cols), F32), []
    for i in range(held):
        gi = gate + g[i * rows : (i + 1) * rows]
        ui = up + u[i * rows : (i + 1) * rows]
        h = (0.5 * gi) * (1.0 + jnp.tanh(0.5 * gi)) * ui
        slot = spot * held + i
        hw = h * weight[:, slot : slot + 1]
        total += hw
        parts.append(hw.astype(BF16))
    back = dot_rows(jnp.concatenate(parts, axis=0), factors[2])
    block = jnp.zeros((rows, rank_cols), F32)
    for i in range(held):
        block += jnp.where(owner == i, back[i * rows : (i + 1) * rows], 0.0)
    return total, block


def hidden_kernel(count, held, place, *refs):
    gs, (low, weight), rs = refs[:count], refs[count : count + 2], refs[count + 2 : 2 * count + 1]
    base, acc, hl = refs[2 * count + 1 :]
    cols = base.shape[1] // 2
    base[...] = sum(g[...].astype(F32) for g in gs)
    total = jnp.zeros(acc.shape, F32)
    for spot, r in enumerate(rs):
        k = spot ^ place[2] if spot == count // 2 else spot
        more, hl[place[0] ^ place[1] ^ k] = expert_terms(
            k, spot, held, place, base[:, :cols], base[:, cols:], low, weight, r
        )
        total += more
    acc[...] = total


def hidden_last_kernel(count, held, place, base, acc, come, low, weight, r, hsum, *refs):
    outs, hl = refs[:-1], refs[-1]
    side = len(outs)
    cols = base.shape[1] // 2
    rank_cols = r.shape[1]
    hl[...] = come[...]
    k = (count - 1) ^ place[2]
    more, hl[place[0] ^ place[1] ^ k] = expert_terms(
        k, count - 1, held, place, base[:, :cols], base[:, cols:], low, weight, r
    )
    hsum[...] = (acc[...] + more).astype(BF16)
    for e in range(side):
        for b in range(side):
            outs[e][:, b * rank_cols : (b + 1) * rank_cols] = hl[side * b + e].astype(outs[e].dtype)


def down_kernel(count, place, hs, w, rd, *refs):
    outs, total = refs[:count], refs[count]
    rows = outs[0].shape[0]
    inner = w.shape[0]
    total[...] = jnp.dot(hs[:, :inner], w[...], preferred_element_type=F32)
    total[...] += jnp.dot(hs[:, inner:], rd[...], preferred_element_type=F32)
    for k in range(count):
        start = pl.multiple_of(lax.rem(place[0] + k, count) * rows, rows)
        outs[k][...] = total[pl.ds(start, rows), :].astype(outs[k].dtype)


VMEM = pl.BlockSpec(memory_space=pltpu.VMEM)
ANY = pl.BlockSpec(memory_space=pl.ANY)
SMEM = pl.BlockSpec(memory_space=pltpu.SMEM)
PARAMS = pltpu.CompilerParams(vmem_limit_bytes=24 * 2**20)

SEP, YR = True, False
TIES = {'C': ['sums0'], 'lowag': ['sums0'], 'far': ['X1', 'X3', 'xe2'], 'mc': ['sent'], 'PLt0': ['sums0'], 'PLt1': ['sums0']}

def stationary_shards(tokens, routes, gate_weights, delta_of, base_gate, base_up, base_down, gate_left, gate_right, up_left, up_right, down_left, down_right):
    count = lax.axis_size("wide")
    rows = tokens.shape[0]
    held, rank = gate_left.shape[0], gate_left.shape[2]
    experts = held * count
    rank_cols = held * rank
    inner = base_gate.shape[1]
    features = base_down.shape[1]
    place = lax.axis_index("wide")
    spot = lax.axis_index("narrow")
    places = jnp.stack([place, spot, lax.axis_index("groups")]).astype(jnp.int32)
    side = math.isqrt(count)
    steps = range(1, count)
    memo, busy = {}, set()

    def get(name):
        if name not in memo:
            assert name not in busy, "cycle"
            busy.add(name)
            memo[name] = nodes[name]()
        return memo[name]

    def tied(a, name):
        deps = [get(d) for d in TIES.get(name, ())]
        return lax.optimization_barrier((a, deps))[0] if deps else a

    def swap(a, k=0):
        pairs = [(i * count + j, (j ^ k) * count + i) for i in range(count) for j in range(count)]
        return lax.ppermute(a, ("wide", "narrow"), pairs)

    def across(a, axis, k):
        return lax.ppermute(a, axis, [(i, i ^ k) for i in range(count)])

    def ahead(a, k):
        return lax.ppermute(a, "wide", [(i, (i + k) % count) for i in range(count)])

    nodes = {}

    def node(f):
        nodes[f.__name__] = f
        return f

    def X(m):
        pairs = [
            (w * count + j, (m ^ (w // side * side + j % side)) * count + j // side * side + w % side)
            for w in range(count)
            for j in range(count)
        ]
        return lax.ppermute(tied(tokens, f"X{m}"), ("wide", "narrow"), pairs)
    for m in range(count):
        nodes[f"X{m}"] = functools.partial(X, m)

    def xe(m):
        pairs = [
            (z * count + n, z * count + (n ^ side))
            for z in range(count)
            for n in range(count)
            if z // side == n // side
        ]
        return lax.ppermute(tied(get(f"X{m}"), f"xe{m}"), ("wide", "narrow"), pairs)
    nodes["xe0"] = lambda: xe(0)
    nodes["xe2"] = lambda: xe(2)

    @node
    def mine():
        holds = spot // side == place // side
        return jnp.concatenate([jnp.where(holds, get(f"X{m}"), get(f"xe{m}")) for m in (0, 2)], axis=0)

    @node
    def mc():
        return across(tied(get("mine"), "mc"), "narrow", 1)

    @node
    def Lp():
        return jnp.concatenate(
            [jnp.swapaxes(a, 1, 2).reshape(rank_cols, a.shape[1]) for a in (gate_left, up_left)], axis=0
        )

    @node
    def Lc():
        return across(tied(get("Lp"), "Lc"), "narrow", 1)

    @node
    def PL():
        spread = [get(f"X{m}") for m in range(count)]
        left = [tied(get("Lp"), "PL"), get("Lc")]
        if SEP:
            return pl.pallas_call(
                functools.partial(left_kernel, count, side),
                out_shape=[jax.ShapeDtypeStruct((rows, 2 * rank_cols), BF16)] * side,
                in_specs=[SMEM] + [VMEM] * (count + side),
                out_specs=[VMEM] * side,
                scratch_shapes=[pltpu.VMEM((count, *tokens.shape), BF16)],
                compiler_params=PARAMS,
            )(places, *spread, *left)
        return pl.pallas_call(
            functools.partial(left_kernel, count, side),
            out_shape=[jax.ShapeDtypeStruct((side * rows, 2 * rank_cols), kind) for kind in (F32, BF16)],
            in_specs=[SMEM] + [VMEM] * (count + side),
            out_specs=[VMEM] * 2,
            scratch_shapes=[pltpu.VMEM((count, *tokens.shape), BF16)],
            compiler_params=PARAMS,
        )(places, *spread, *left)

    @node
    def sent():
        return get("PL")[1]

    @node
    def PLt0():
        return swap(tied(get("PL")[0], "PLt0"), 0)

    @node
    def PLt1():
        return swap(tied(get("PL")[1], "PLt1"), side)

    @node
    def PLx():
        return across(tied(get("PL")[1], "PLx"), "narrow", side)

    @node
    def low():
        if SEP:
            return (get("PLt0").astype(F32) + get("PLt1").astype(F32)).astype(BF16)
        return (get("PL")[0] + get("PLx").astype(F32)).astype(BF16)

    @node
    def PLc():
        return across(tied(get("low"), "PLc"), "narrow", 1)

    @node
    def lowag():
        return lax.all_gather(tied(get("low"), "lowag"), "narrow", axis=0, tiled=True)

    @node
    def Rp():
        return jnp.stack(
            [
                gate_right.reshape(rank_cols, inner),
                up_right.reshape(rank_cols, inner),
                jnp.swapaxes(down_left, 1, 2).reshape(rank_cols, inner),
            ]
        )

    @node
    def part():
        if not YR:
            return get("Rp")
        half = rank_cols // 2
        return lax.dynamic_slice_in_dim(get("Rp"), lax.axis_index("groups") * half, half, axis=1)

    @node
    def far():
        pairs = [(g * count + z, g * count + (z ^ 2 ^ g)) for g in range(2) for z in range(count)]
        return lax.ppermute(tied(get("part"), "far"), ("groups", "wide"), pairs)

    @node
    def near():
        return across(tied(get("part"), "near"), "wide", 1)

    @node
    def C():
        return lax.ppermute(tied(get("far"), "C"), "groups", [(0, 1), (1, 0)])

    @node
    def close():
        return across(jnp.stack([get("part"), tied(get("far"), "close")]), "wide", 1)

    @node
    def brought():
        return jnp.stack([get("close")[0], get("far"), get("close")[1]])

    @node
    def Y():
        return lax.ppermute(tied(get("brought"), "Y"), "groups", [(0, 1), (1, 0)])

    @node
    def mm1():
        own = [tied(get("mine"), "mm1"), get("mc")]
        if SEP:
            return pl.pallas_call(
                functools.partial(base_kernel, count, side),
                out_shape=[jax.ShapeDtypeStruct((rows, 2 * inner), F32 if k == 0 else BF16) for k in range(count)],
                in_specs=[SMEM] + [VMEM] * (side + 2),
                out_specs=[VMEM] * count,
                scratch_shapes=[pltpu.VMEM((count * rows, 2 * inner), F32)],
                compiler_params=PARAMS,
            )(places, *own, base_gate, base_up)
        wide_cols = 2 * inner + 2 * rank_cols
        return pl.pallas_call(
            functools.partial(base_kernel, count, side),
            out_shape=[jax.ShapeDtypeStruct((rows, wide_cols), F32 if k == 0 else BF16) for k in range(count)],
            in_specs=[SMEM] + [VMEM] * (2 * side + 2),
            out_specs=[VMEM] * count,
            scratch_shapes=[
                pltpu.VMEM((count * rows, 2 * inner), F32),
                pltpu.VMEM((count * rows, 2 * rank_cols), BF16),
            ],
            compiler_params=PARAMS,
        )(places, *own, get("low"), get("PLc"), base_gate, base_up)

    @node
    def sums0():
        return get("mm1")[0]

    for k in range(1, count):
        nodes[f"P{k}"] = lambda k=k: across(tied(get("mm1")[k], f"P{k}"), "wide", k)

    @node
    def weight():
        expert_ids = lax.broadcasted_iota(jnp.int32, (1, 1, experts), 2)
        named = routes[:, :, None] == expert_ids
        delta_ids = jnp.sum(jnp.where(named, delta_of[None, None, :], 0), axis=2)
        away = (delta_ids // held) ^ place
        away = jnp.where(away < 2, away, away ^ lax.axis_index("groups"))
        slots = away * held + delta_ids % held
        return jnp.sum(jnp.where(slots[:, :, None] == expert_ids, gate_weights[:, :, None], 0.0), axis=1)

    for name in ['C']:
        get(name)
    sums = [get("sums0")] + [get(f"P{k}") for k in steps]
    extra = [get("lowag")] if SEP else []
    if YR:
        fac = [get("Rp"), get("brought"), get("Y")]
        more = [pltpu.VMEM((count - 1, *get("Rp").shape), BF16)]
    else:
        fac = [get("Rp"), get("near"), get("far"), get("C")]
        more = []
    ins = [places, *sums, *extra, get("weight"), *fac]
    base, acc, hl = pl.pallas_call(
        functools.partial(hidden_kernel, count, held),
        out_shape=[
            jax.ShapeDtypeStruct((rows, 2 * inner), F32),
            jax.ShapeDtypeStruct((rows, inner), F32),
            jax.ShapeDtypeStruct((count, rows, rank_cols), F32),
        ],
        in_specs=[SMEM] + [VMEM] * (2 * count + 1),
        out_specs=[VMEM] * 3,
        compiler_params=PARAMS,
    )(places, *sums, get("lowag"), get("weight"), *fac[:-1])
    hsum, *parts = pl.pallas_call(
        functools.partial(hidden_last_kernel, count, held),
        out_shape=[jax.ShapeDtypeStruct((rows, inner), BF16)]
        + [jax.ShapeDtypeStruct((rows, side * rank_cols), F32 if e == 0 else BF16) for e in range(side)],
        in_specs=[SMEM] + [VMEM] * 6,
        out_specs=[VMEM] * (side + 1),
        scratch_shapes=[pltpu.VMEM((count, rows, rank_cols), F32)],
        compiler_params=PARAMS,
    )(places, base, acc, hl, get("lowag"), get("weight"), fac[-1])
    part = parts[0] + sum(across(parts[e], "narrow", e).astype(F32) for e in range(1, side))
    part = jnp.split(part.astype(BF16), side, axis=1)
    first = swap(jnp.concatenate([hsum, part[0]], axis=1))
    low_sum = first[:, inner:].astype(F32) + sum(swap(part[b], side * b).astype(F32) for b in range(1, side))
    hs = jnp.concatenate([first[:, :inner], low_sum.astype(BF16)], axis=1)
    hs = lax.all_gather(hs, "narrow", axis=0, tiled=True)
    outs = pl.pallas_call(
        functools.partial(down_kernel, count),
        out_shape=[jax.ShapeDtypeStruct((rows, features), F32 if k == 0 else BF16) for k in range(count)],
        in_specs=[SMEM] + [VMEM] * 3,
        out_specs=[VMEM] * count,
        scratch_shapes=[pltpu.VMEM((count * rows, features), F32)],
        compiler_params=PARAMS,
    )(places, hs, base_down, down_right.reshape(rank_cols, features))
    return sum([outs[0]] + [ahead(outs[k], k).astype(F32) for k in steps]).astype(BF16)


def solution(mesh):
    count = mesh.shape["wide"]
    square = count == mesh.shape["narrow"] == math.isqrt(count) ** 2 and count & (count - 1) == 0
    return jax.shard_map(
        stationary_shards if square else gathered_shards,
        mesh=mesh,
        in_specs=(
            P(("groups", "wide"), "narrow"),
            P(("groups", "wide"), None),
            P(("groups", "wide"), None),
            P(),
            P("wide", "narrow"),
            P("wide", "narrow"),
            P("wide", "narrow"),
            P("wide", "narrow", None),
            P("wide", None, "narrow"),
            P("wide", "narrow", None),
            P("wide", None, "narrow"),
            P("wide", "narrow", None),
            P("wide", None, "narrow"),
        ),
        out_specs=P(("groups", "wide"), "narrow"),
        check_vma=False,
    )
```

```python
import functools
import math

import jax
import jax.numpy as jnp
from jax import lax
from jax.experimental import pallas as pl
from jax.experimental.pallas import tpu as pltpu
from jax.sharding import PartitionSpec as P

F32 = jnp.float32
BF16 = jnp.bfloat16


def with_zero_row(rows):
    return jnp.concatenate([rows, jnp.zeros((1, rows.shape[1]), rows.dtype)], axis=0)


def rebuild(base_rows, left_rows, right_factor):
    product = jnp.einsum(
        "ecr,erf->ecf", left_rows, right_factor, preferred_element_type=jnp.float32
    )
    return (base_rows.astype(jnp.float32)[None] + product).astype(jnp.bfloat16)


def gathered_shards(
    tokens,
    routes,
    gate_weights,
    delta_of,
    base_gate,
    base_up,
    base_down,
    gate_left,
    gate_right,
    up_left,
    up_right,
    down_left,
    down_right,
):
    block_rows, top_count = routes.shape
    feature_part = tokens.shape[1]
    exp_here = gate_left.shape[0]
    wide_count = lax.axis_size("wide")
    experts = wide_count * exp_here
    capacity = max(2, block_rows * top_count * 5 // (4 * experts))
    slot_total = experts * capacity
    expert_ids = lax.broadcasted_iota(jnp.int32, (1, 1, experts), 2)
    onehot = (routes[:, :, None] == expert_ids).astype(jnp.float32)
    routed = jnp.sum(onehot, axis=1)
    row_index = lax.broadcasted_iota(jnp.int32, (block_rows, block_rows), 0)
    col_index = lax.broadcasted_iota(jnp.int32, (block_rows, block_rows), 1)
    earlier_mask = (col_index < row_index).astype(jnp.float32)
    before = jnp.dot(
        earlier_mask, routed, preferred_element_type=jnp.float32, precision=lax.Precision.HIGHEST
    )
    place_in = jnp.sum(onehot * before[:, None, :], axis=2).astype(jnp.int32)
    delta_ids = jnp.sum(onehot * delta_of.astype(jnp.float32)[None, None, :], axis=2).astype(
        jnp.int32
    )
    position = delta_ids * capacity + place_in
    every_row = lax.all_gather(tokens, "wide", axis=0, tiled=True)
    every_place = lax.all_gather(position, "wide", axis=0, tiled=True)
    own_first = lax.axis_index("wide") * (exp_here * capacity)
    local_place = every_place - own_first
    owned = (local_place >= 0) & (local_place < exp_here * capacity)
    block_ids = lax.broadcasted_iota(jnp.int32, every_place.shape, 0) // block_rows
    target = jnp.where(owned, block_ids * (exp_here * capacity) + local_place, slot_total)
    every_token = lax.broadcasted_iota(jnp.int32, every_place.shape, 0)
    picked_rows = (
        jnp.full((slot_total,), every_row.shape[0], jnp.int32)
        .at[target.reshape(-1)]
        .set(every_token.reshape(-1), mode="drop")
    )
    local_rows = jnp.take(with_zero_row(every_row), picked_rows, axis=0).reshape(
        wide_count, exp_here, capacity, feature_part
    )
    slot_rows = lax.all_gather(local_rows, "narrow", axis=3, tiled=True)
    left_gate, left_up, left_down = (
        lax.all_gather(gate_left, "narrow", axis=1, tiled=True),
        lax.all_gather(up_left, "narrow", axis=1, tiled=True),
        lax.all_gather(down_left, "narrow", axis=1, tiled=True),
    )
    base_rows_gate = lax.all_gather(base_gate, "wide", axis=0, tiled=True)
    base_rows_up = lax.all_gather(base_up, "wide", axis=0, tiled=True)
    columns = slot_rows
    dense_gate = rebuild(base_rows_gate, left_gate, gate_right)
    dense_up = rebuild(base_rows_up, left_up, up_right)
    gate_sum = jnp.einsum("secd,edf->secf", columns, dense_gate, preferred_element_type=jnp.float32)
    up_sum = jnp.einsum("secd,edf->secf", columns, dense_up, preferred_element_type=jnp.float32)
    hidden = (jax.nn.silu(gate_sum) * up_sum).astype(jnp.bfloat16)
    hidden_all = lax.all_gather(hidden, "narrow", axis=3, tiled=True)
    dense_down = rebuild(
        lax.all_gather(base_down, "wide", axis=0, tiled=True), left_down, down_right
    )
    columns = hidden_all
    expert_out = jnp.einsum(
        "secf,efd->secd", columns, dense_down, preferred_element_type=jnp.float32
    ).astype(jnp.bfloat16)
    returned = lax.all_to_all(expert_out, "wide", split_axis=0, concat_axis=0, tiled=True).reshape(
        slot_total, feature_part
    )
    picked = jnp.take(returned, position.reshape(-1), axis=0).reshape(
        block_rows, top_count, feature_part
    )
    mixed_out = jnp.sum(gate_weights[:, :, None] * picked.astype(jnp.float32), axis=1)
    return mixed_out.astype(jnp.bfloat16)


def dot_rows(a, b):
    return lax.dot_general(a, b, (((1,), (1,)), ((), ())), preferred_element_type=F32)


def left_kernel(count, side, place, *refs):
    xs, ls, (out, sent, held) = refs[:count], refs[count : count + side], refs[count + side :]
    rows = xs[0].shape[0]
    for m in range(count):
        held[m] = xs[m][...]
    total = jnp.zeros(out.shape, F32)
    for e in range(side):
        spots = [place[0] ^ (side * u + (lax.rem(place[1], side) ^ e)) for u in range(side)]
        total += dot_rows(jnp.concatenate([held[m] for m in spots], axis=0), ls[e][...])
    out[...] = total
    sent[...] = total.astype(BF16)


def base_kernel(count, side, place, *refs):
    xs, lows, (wg, wu), refs = refs[:side], refs[side : 2 * side], refs[2 * side : 2 * side + 2], refs[2 * side + 2 :]
    outs, (total, low) = refs[:-2], refs[-2:]
    cols = wg.shape[1]
    rows = outs[0].shape[0]
    x = jnp.concatenate([x[...] for x in xs], axis=0)
    total[:, :cols] = jnp.dot(x, wg[...], preferred_element_type=F32)
    total[:, cols:] = jnp.dot(x, wu[...], preferred_element_type=F32)
    low[...] = jnp.concatenate([low[...] for low in lows], axis=0)
    for k in range(count):
        turn = lax.rem(place[0] ^ place[1] ^ k, side)
        start = pl.multiple_of((turn * side + k // side) * rows, rows)
        outs[k][:, : 2 * cols] = total[pl.ds(start, rows), :].astype(outs[k].dtype)
        start = pl.multiple_of((turn * side + ((place[0] ^ k) // side)) * rows, rows)
        outs[k][:, 2 * cols :] = low[pl.ds(start, rows), :].astype(outs[k].dtype)


def expert_terms(k, spot, held, place, gate, up, low, weight, factors):
    rows, cols = gate.shape
    rank_cols = factors.shape[1]
    owner = lax.broadcasted_iota(jnp.int32, (rows, rank_cols), 1) // (rank_cols // held)
    here = low[k]
    sides = []
    for half in (here[:, :rank_cols], here[:, rank_cols:]):
        zero = jnp.zeros_like(half)
        sides.append(jnp.concatenate([jnp.where(owner == i, half, zero) for i in range(held)], axis=0))
    g = jnp.dot(sides[0], factors[0], preferred_element_type=F32)
    u = jnp.dot(sides[1], factors[1], preferred_element_type=F32)
    total, parts = jnp.zeros((rows, cols), F32), []
    for i in range(held):
        gi = gate + g[i * rows : (i + 1) * rows]
        ui = up + u[i * rows : (i + 1) * rows]
        h = (gi / (1.0 + jnp.exp(-gi))) * ui
        slot = spot * held + i
        hw = h * weight[:, slot : slot + 1]
        total += hw
        parts.append(hw.astype(BF16))
    back = dot_rows(jnp.concatenate(parts, axis=0), factors[2])
    block = jnp.zeros((rows, rank_cols), F32)
    for i in range(held):
        block += jnp.where(owner == i, back[i * rows : (i + 1) * rows], 0.0)
    return total, block


def hidden_kernel(count, held, place, *refs):
    gs, weight, rs = refs[:count], refs[count], refs[count + 1 : 2 * count]
    base, acc, hl, low = refs[2 * count :]
    cols = base.shape[1] // 2
    base[...] = sum(g[:, : 2 * cols].astype(F32) for g in gs)
    for k, g in enumerate(gs):
        low[k] = g[:, 2 * cols :].astype(BF16)
    total = jnp.zeros(acc.shape, F32)
    for spot, r in enumerate(rs):
        k = spot ^ place[2] if spot == count // 2 else spot
        more, hl[place[0] ^ place[1] ^ k] = expert_terms(
            k, spot, held, place, base[:, :cols], base[:, cols:], low, weight, r
        )
        total += more
    acc[...] = total


def hidden_last_kernel(count, held, place, base, acc, come, low, weight, r, hsum, *refs):
    outs, hl = refs[:-1], refs[-1]
    side = len(outs)
    cols = base.shape[1] // 2
    rank_cols = r.shape[1]
    hl[...] = come[...]
    k = (count - 1) ^ place[2]
    more, hl[place[0] ^ place[1] ^ k] = expert_terms(
        k, count - 1, held, place, base[:, :cols], base[:, cols:], low, weight, r
    )
    hsum[...] = (acc[...] + more).astype(BF16)
    for e in range(side):
        for b in range(side):
            outs[e][:, b * rank_cols : (b + 1) * rank_cols] = hl[side * b + e].astype(outs[e].dtype)


def down_kernel(count, place, hs, w, rd, *refs):
    outs, total = refs[:count], refs[count]
    rows = outs[0].shape[0]
    inner = w.shape[0]
    total[...] = jnp.dot(hs[:, :inner], w[...], preferred_element_type=F32)
    total[...] += jnp.dot(hs[:, inner:], rd[...], preferred_element_type=F32)
    for k in range(count):
        start = pl.multiple_of(lax.rem(place[0] + k, count) * rows, rows)
        outs[k][...] = total[pl.ds(start, rows), :].astype(outs[k].dtype)


VMEM = pl.BlockSpec(memory_space=pltpu.VMEM)
SMEM = pl.BlockSpec(memory_space=pltpu.SMEM)
PARAMS = pltpu.CompilerParams(vmem_limit_bytes=24 * 2**20)


def after(a, *others):
    return lax.optimization_barrier((a, others))[0]


def stationary_shards(
    tokens,
    routes,
    gate_weights,
    delta_of,
    base_gate,
    base_up,
    base_down,
    gate_left,
    gate_right,
    up_left,
    up_right,
    down_left,
    down_right,
):
    count = lax.axis_size("wide")
    side = math.isqrt(count)
    rows = tokens.shape[0]
    held, rank = gate_left.shape[0], gate_left.shape[2]
    experts = held * count
    rank_cols = held * rank
    inner = base_gate.shape[1]
    features = base_down.shape[1]
    place, spot, group = (lax.axis_index(a) for a in ("wide", "narrow", "groups"))
    places = jnp.stack([place, spot, group]).astype(jnp.int32)

    def swap(a, k=0):
        pairs = [(i * count + j, (j ^ k) * count + i) for i in range(count) for j in range(count)]
        return lax.ppermute(a, ("wide", "narrow"), pairs)

    def across(a, axis, k):
        return lax.ppermute(a, axis, [(i, i ^ k) for i in range(count)])

    def ahead(a, k):
        return lax.ppermute(a, "wide", [(i, (i + k) % count) for i in range(count)])

    spread = []
    for m in range(count):
        pairs = [
            (w * count + j, (m ^ (w // side * side + j % side)) * count + j // side * side + w % side)
            for w in range(count)
            for j in range(count)
        ]
        spread.append(lax.ppermute(tokens, ("wide", "narrow"), pairs))

    pairs = [
        (z * count + n, z * count + (n ^ side))
        for z in range(count)
        for n in range(count)
        if z // side == n // side
    ]
    come = [lax.ppermute(spread[side * a], ("wide", "narrow"), pairs) for a in range(side)]
    holds = spot // side == place // side
    mine = jnp.concatenate([jnp.where(holds, spread[side * a], come[a]) for a in range(side)], axis=0)

    left = jnp.concatenate(
        [jnp.swapaxes(a, 1, 2).reshape(rank_cols, a.shape[1]) for a in (gate_left, up_left)], axis=0
    )
    low, sent = pl.pallas_call(
        functools.partial(left_kernel, count, side),
        out_shape=[jax.ShapeDtypeStruct((side * rows, 2 * rank_cols), kind) for kind in (F32, BF16)],
        in_specs=[SMEM] + [VMEM] * (count + side),
        out_specs=[VMEM] * 2,
        scratch_shapes=[pltpu.VMEM((count, *tokens.shape), BF16)],
        compiler_params=PARAMS,
    )(places, *spread, left, across(left, "narrow", 1))
    low = (low + across(sent, "narrow", side).astype(F32)).astype(BF16)

    wide_cols = 2 * inner + 2 * rank_cols
    sums = pl.pallas_call(
        functools.partial(base_kernel, count, side),
        out_shape=[jax.ShapeDtypeStruct((rows, wide_cols), F32 if k == 0 else BF16) for k in range(count)],
        in_specs=[SMEM] + [VMEM] * (2 * side + 2),
        out_specs=[VMEM] * count,
        scratch_shapes=[
            pltpu.VMEM((count * rows, 2 * inner), F32),
            pltpu.VMEM((count * rows, 2 * rank_cols), BF16),
        ],
        compiler_params=PARAMS,
    )(
        places,
        mine,
        across(after(mine, sent), "narrow", 1),
        low,
        across(low, "narrow", 1),
        base_gate,
        base_up,
    )

    own = jnp.stack(
        [
            gate_right.reshape(rank_cols, inner),
            up_right.reshape(rank_cols, inner),
            jnp.swapaxes(down_left, 1, 2).reshape(rank_cols, inner),
        ]
    )
    pairs = [(g * count + z, g * count + (z ^ 2 ^ g)) for g in range(2) for z in range(count)]
    far = lax.ppermute(after(own, spread[1], spread[3], come[1]), ("groups", "wide"), pairs)
    traded = lax.ppermute(after(far, sums[0]), "groups", [(0, 1), (1, 0)])
    sums = [sums[0]] + [across(sums[k], "wide", k) for k in range(1, count)]
    near = across(own, "wide", 1)

    expert_ids = lax.broadcasted_iota(jnp.int32, (1, 1, experts), 2)
    named = routes[:, :, None] == expert_ids
    delta_ids = jnp.sum(jnp.where(named, delta_of[None, None, :], 0), axis=2)
    away = (delta_ids // held) ^ place
    away = jnp.where(away < 2, away, away ^ group)
    slots = away * held + delta_ids % held
    weight = jnp.sum(jnp.where(slots[:, :, None] == expert_ids, gate_weights[:, :, None], 0.0), axis=1)

    base, acc, hl, low = pl.pallas_call(
        functools.partial(hidden_kernel, count, held),
        out_shape=[
            jax.ShapeDtypeStruct((rows, 2 * inner), F32),
            jax.ShapeDtypeStruct((rows, inner), F32),
            jax.ShapeDtypeStruct((count, rows, rank_cols), F32),
            jax.ShapeDtypeStruct((count, rows, 2 * rank_cols), BF16),
        ],
        in_specs=[SMEM] + [VMEM] * (2 * count),
        out_specs=[VMEM] * 4,
        compiler_params=PARAMS,
    )(places, *sums, weight, own, near, far)
    hsum, kept, given = pl.pallas_call(
        functools.partial(hidden_last_kernel, count, held),
        out_shape=[
            jax.ShapeDtypeStruct((rows, inner), BF16),
            jax.ShapeDtypeStruct((rows, side * rank_cols), F32),
            jax.ShapeDtypeStruct((rows, side * rank_cols), BF16),
        ],
        in_specs=[SMEM] + [VMEM] * 6,
        out_specs=[VMEM] * 3,
        scratch_shapes=[pltpu.VMEM((count, rows, rank_cols), F32)],
        compiler_params=PARAMS,
    )(places, base, acc, hl, low, weight, traded)

    part = (kept + across(given, "narrow", 1).astype(F32)).astype(BF16)
    part = jnp.split(part, side, axis=1)
    first = swap(jnp.concatenate([hsum, part[0]], axis=1))
    low_sum = first[:, inner:].astype(F32) + sum(swap(part[b], side * b).astype(F32) for b in range(1, side))
    hs = jnp.concatenate([first[:, :inner], low_sum.astype(BF16)], axis=1)
    hs = lax.all_gather(hs, "narrow", axis=0, tiled=True)
    outs = pl.pallas_call(
        functools.partial(down_kernel, count),
        out_shape=[jax.ShapeDtypeStruct((rows, features), F32 if k == 0 else BF16) for k in range(count)],
        in_specs=[SMEM] + [VMEM] * 3,
        out_specs=[VMEM] * count,
        scratch_shapes=[pltpu.VMEM((count * rows, features), F32)],
        compiler_params=PARAMS,
    )(places, hs, base_down, down_right.reshape(rank_cols, features))
    return sum([outs[0]] + [ahead(outs[k], k).astype(F32) for k in range(1, count)]).astype(BF16)


def solution(mesh):
    shape = mesh.shape
    stationary = shape["groups"] == 2 and shape["wide"] == shape["narrow"] == shape["groups"] ** 2
    return jax.shard_map(
        stationary_shards if stationary else gathered_shards,
        mesh=mesh,
        in_specs=(
            P(("groups", "wide"), "narrow"),
            P(("groups", "wide"), None),
            P(("groups", "wide"), None),
            P(),
            P("wide", "narrow"),
            P("wide", "narrow"),
            P("wide", "narrow"),
            P("wide", "narrow", None),
            P("wide", None, "narrow"),
            P("wide", "narrow", None),
            P("wide", None, "narrow"),
            P("wide", "narrow", None),
            P("wide", None, "narrow"),
        ),
        out_specs=P(("groups", "wide"), "narrow"),
        check_vma=False,
    )
```

```python
import functools
import math

import jax
import jax.numpy as jnp
from jax import lax
from jax.experimental import pallas as pl
from jax.experimental.pallas import tpu as pltpu
from jax.sharding import PartitionSpec as P

F32 = jnp.float32
BF16 = jnp.bfloat16


def with_zero_row(rows):
    return jnp.concatenate([rows, jnp.zeros((1, rows.shape[1]), rows.dtype)], axis=0)


def rebuild(base_rows, left_rows, right_factor):
    product = jnp.einsum(
        "ecr,erf->ecf", left_rows, right_factor, preferred_element_type=jnp.float32
    )
    return (base_rows.astype(jnp.float32)[None] + product).astype(jnp.bfloat16)


def gathered_shards(
    tokens,
    routes,
    gate_weights,
    delta_of,
    base_gate,
    base_up,
    base_down,
    gate_left,
    gate_right,
    up_left,
    up_right,
    down_left,
    down_right,
):
    block_rows, top_count = routes.shape
    feature_part = tokens.shape[1]
    exp_here = gate_left.shape[0]
    wide_count = lax.axis_size("wide")
    experts = wide_count * exp_here
    capacity = max(2, block_rows * top_count * 5 // (4 * experts))
    slot_total = experts * capacity
    expert_ids = lax.broadcasted_iota(jnp.int32, (1, 1, experts), 2)
    onehot = (routes[:, :, None] == expert_ids).astype(jnp.float32)
    routed = jnp.sum(onehot, axis=1)
    row_index = lax.broadcasted_iota(jnp.int32, (block_rows, block_rows), 0)
    col_index = lax.broadcasted_iota(jnp.int32, (block_rows, block_rows), 1)
    earlier_mask = (col_index < row_index).astype(jnp.float32)
    before = jnp.dot(
        earlier_mask, routed, preferred_element_type=jnp.float32, precision=lax.Precision.HIGHEST
    )
    place_in = jnp.sum(onehot * before[:, None, :], axis=2).astype(jnp.int32)
    delta_ids = jnp.sum(onehot * delta_of.astype(jnp.float32)[None, None, :], axis=2).astype(
        jnp.int32
    )
    position = delta_ids * capacity + place_in
    every_row = lax.all_gather(tokens, "wide", axis=0, tiled=True)
    every_place = lax.all_gather(position, "wide", axis=0, tiled=True)
    own_first = lax.axis_index("wide") * (exp_here * capacity)
    local_place = every_place - own_first
    owned = (local_place >= 0) & (local_place < exp_here * capacity)
    block_ids = lax.broadcasted_iota(jnp.int32, every_place.shape, 0) // block_rows
    target = jnp.where(owned, block_ids * (exp_here * capacity) + local_place, slot_total)
    every_token = lax.broadcasted_iota(jnp.int32, every_place.shape, 0)
    picked_rows = (
        jnp.full((slot_total,), every_row.shape[0], jnp.int32)
        .at[target.reshape(-1)]
        .set(every_token.reshape(-1), mode="drop")
    )
    local_rows = jnp.take(with_zero_row(every_row), picked_rows, axis=0).reshape(
        wide_count, exp_here, capacity, feature_part
    )
    slot_rows = lax.all_gather(local_rows, "narrow", axis=3, tiled=True)
    left_gate, left_up, left_down = (
        lax.all_gather(gate_left, "narrow", axis=1, tiled=True),
        lax.all_gather(up_left, "narrow", axis=1, tiled=True),
        lax.all_gather(down_left, "narrow", axis=1, tiled=True),
    )
    base_rows_gate = lax.all_gather(base_gate, "wide", axis=0, tiled=True)
    base_rows_up = lax.all_gather(base_up, "wide", axis=0, tiled=True)
    columns = slot_rows
    dense_gate = rebuild(base_rows_gate, left_gate, gate_right)
    dense_up = rebuild(base_rows_up, left_up, up_right)
    gate_sum = jnp.einsum("secd,edf->secf", columns, dense_gate, preferred_element_type=jnp.float32)
    up_sum = jnp.einsum("secd,edf->secf", columns, dense_up, preferred_element_type=jnp.float32)
    hidden = (jax.nn.silu(gate_sum) * up_sum).astype(jnp.bfloat16)
    hidden_all = lax.all_gather(hidden, "narrow", axis=3, tiled=True)
    dense_down = rebuild(
        lax.all_gather(base_down, "wide", axis=0, tiled=True), left_down, down_right
    )
    columns = hidden_all
    expert_out = jnp.einsum(
        "secf,efd->secd", columns, dense_down, preferred_element_type=jnp.float32
    ).astype(jnp.bfloat16)
    returned = lax.all_to_all(expert_out, "wide", split_axis=0, concat_axis=0, tiled=True).reshape(
        slot_total, feature_part
    )
    picked = jnp.take(returned, position.reshape(-1), axis=0).reshape(
        block_rows, top_count, feature_part
    )
    mixed_out = jnp.sum(gate_weights[:, :, None] * picked.astype(jnp.float32), axis=1)
    return mixed_out.astype(jnp.bfloat16)


def dot_rows(a, b):
    return lax.dot_general(a, b, (((1,), (1,)), ((), ())), preferred_element_type=F32)


def left_kernel(count, side, place, *refs):
    xs, ls, (out, sent, held) = refs[:count], refs[count : count + side], refs[count + side :]
    rows = xs[0].shape[0]
    for m in range(count):
        held[m] = xs[m][...]
    total = jnp.zeros(out.shape, F32)
    for e in range(side):
        spots = [place[0] ^ (side * u + (lax.rem(place[1], side) ^ e)) for u in range(side)]
        total += dot_rows(jnp.concatenate([held[m] for m in spots], axis=0), ls[e][...])
    out[...] = total
    sent[...] = total.astype(BF16)


def base_kernel(count, side, place, *refs):
    xs, lows, (wg, wu), refs = refs[:side], refs[side : 2 * side], refs[2 * side : 2 * side + 2], refs[2 * side + 2 :]
    outs, (total, low) = refs[:-2], refs[-2:]
    cols = wg.shape[1]
    rows = outs[0].shape[0]
    x = jnp.concatenate([x[...] for x in xs], axis=0)
    total[:, :cols] = jnp.dot(x, wg[...], preferred_element_type=F32)
    total[:, cols:] = jnp.dot(x, wu[...], preferred_element_type=F32)
    low[...] = jnp.concatenate([low[...] for low in lows], axis=0)
    for k in range(count):
        turn = lax.rem(place[0] ^ place[1] ^ k, side)
        start = pl.multiple_of((turn * side + k // side) * rows, rows)
        outs[k][:, : 2 * cols] = total[pl.ds(start, rows), :].astype(outs[k].dtype)
        start = pl.multiple_of((turn * side + ((place[0] ^ k) // side)) * rows, rows)
        outs[k][:, 2 * cols :] = low[pl.ds(start, rows), :].astype(outs[k].dtype)


def expert_terms(k, spot, held, place, gate, up, low, weight, factors):
    rows, cols = gate.shape
    rank_cols = factors.shape[1]
    owner = lax.broadcasted_iota(jnp.int32, (rows, rank_cols), 1) // (rank_cols // held)
    here = low[k]
    sides = []
    for half in (here[:, :rank_cols], here[:, rank_cols:]):
        zero = jnp.zeros_like(half)
        sides.append(jnp.concatenate([jnp.where(owner == i, half, zero) for i in range(held)], axis=0))
    g = jnp.dot(sides[0], factors[0], preferred_element_type=F32)
    u = jnp.dot(sides[1], factors[1], preferred_element_type=F32)
    total, parts = jnp.zeros((rows, cols), F32), []
    for i in range(held):
        gi = gate + g[i * rows : (i + 1) * rows]
        ui = up + u[i * rows : (i + 1) * rows]
        h = (gi / (1.0 + jnp.exp(-gi))) * ui
        slot = spot * held + i
        hw = h * weight[:, slot : slot + 1]
        total += hw
        parts.append(hw.astype(BF16))
    back = dot_rows(jnp.concatenate(parts, axis=0), factors[2])
    block = jnp.zeros((rows, rank_cols), F32)
    for i in range(held):
        block += jnp.where(owner == i, back[i * rows : (i + 1) * rows], 0.0)
    return total, block


def hidden_kernel(count, held, place, *refs):
    gs, weight, rs = refs[:count], refs[count], refs[count + 1 : 2 * count]
    base, acc, hl, low = refs[2 * count :]
    cols = base.shape[1] // 2
    base[...] = sum(g[:, : 2 * cols].astype(F32) for g in gs)
    for k, g in enumerate(gs):
        low[k] = g[:, 2 * cols :].astype(BF16)
    total = jnp.zeros(acc.shape, F32)
    for spot, r in enumerate(rs):
        k = spot ^ place[2] if spot == count // 2 else spot
        more, hl[place[0] ^ place[1] ^ k] = expert_terms(
            k, spot, held, place, base[:, :cols], base[:, cols:], low, weight, r
        )
        total += more
    acc[...] = total


def hidden_last_kernel(count, held, place, base, acc, come, low, weight, r, hsum, *refs):
    outs, hl = refs[:-1], refs[-1]
    side = len(outs)
    cols = base.shape[1] // 2
    rank_cols = r.shape[1]
    hl[...] = come[...]
    k = (count - 1) ^ place[2]
    more, hl[place[0] ^ place[1] ^ k] = expert_terms(
        k, count - 1, held, place, base[:, :cols], base[:, cols:], low, weight, r
    )
    hsum[...] = (acc[...] + more).astype(BF16)
    for e in range(side):
        for b in range(side):
            outs[e][:, b * rank_cols : (b + 1) * rank_cols] = hl[side * b + e].astype(outs[e].dtype)


def down_kernel(count, side, place, mine, other, w, rd, *refs):
    outs, total = refs[:count], refs[count]
    rows = outs[0].shape[0]
    inner = w.shape[0]
    hs = jnp.concatenate([mine[...], other[...]], axis=0)
    total[...] = jnp.dot(hs[:, :inner], w[...], preferred_element_type=F32)
    total[...] += jnp.dot(hs[:, inner:], rd[...], preferred_element_type=F32)
    for k in range(count):
        away = lax.rem(place[0] + k, count) ^ place[1]
        start = pl.multiple_of((lax.rem(away, side) * side + away // side) * rows, rows)
        outs[k][...] = total[pl.ds(start, rows), :].astype(outs[k].dtype)


VMEM = pl.BlockSpec(memory_space=pltpu.VMEM)
SMEM = pl.BlockSpec(memory_space=pltpu.SMEM)
PARAMS = pltpu.CompilerParams(vmem_limit_bytes=24 * 2**20)


def after(a, *others):
    return lax.optimization_barrier((a, others))[0]


def stationary_shards(
    tokens,
    routes,
    gate_weights,
    delta_of,
    base_gate,
    base_up,
    base_down,
    gate_left,
    gate_right,
    up_left,
    up_right,
    down_left,
    down_right,
):
    count = lax.axis_size("wide")
    side = math.isqrt(count)
    rows = tokens.shape[0]
    held, rank = gate_left.shape[0], gate_left.shape[2]
    experts = held * count
    rank_cols = held * rank
    inner = base_gate.shape[1]
    features = base_down.shape[1]
    place, spot, group = (lax.axis_index(a) for a in ("wide", "narrow", "groups"))
    places = jnp.stack([place, spot, group]).astype(jnp.int32)

    def swap(a, k=0):
        pairs = [(i * count + j, (j ^ k) * count + i) for i in range(count) for j in range(count)]
        return lax.ppermute(a, ("wide", "narrow"), pairs)

    def across(a, axis, k):
        return lax.ppermute(a, axis, [(i, i ^ k) for i in range(count)])

    def ahead(a, k):
        return lax.ppermute(a, "wide", [(i, (i + k) % count) for i in range(count)])

    spread = []
    for m in range(count):
        pairs = [
            (w * count + j, (m ^ (w // side * side + j % side)) * count + j // side * side + w % side)
            for w in range(count)
            for j in range(count)
        ]
        spread.append(lax.ppermute(tokens, ("wide", "narrow"), pairs))

    pairs = [
        (z * count + n, z * count + (n ^ side))
        for z in range(count)
        for n in range(count)
        if z // side == n // side
    ]
    come = [lax.ppermute(spread[side * a], ("wide", "narrow"), pairs) for a in range(side)]
    holds = spot // side == place // side
    mine = jnp.concatenate([jnp.where(holds, spread[side * a], come[a]) for a in range(side)], axis=0)

    left = jnp.concatenate(
        [jnp.swapaxes(a, 1, 2).reshape(rank_cols, a.shape[1]) for a in (gate_left, up_left)], axis=0
    )
    low, sent = pl.pallas_call(
        functools.partial(left_kernel, count, side),
        out_shape=[jax.ShapeDtypeStruct((side * rows, 2 * rank_cols), kind) for kind in (F32, BF16)],
        in_specs=[SMEM] + [VMEM] * (count + side),
        out_specs=[VMEM] * 2,
        scratch_shapes=[pltpu.VMEM((count, *tokens.shape), BF16)],
        compiler_params=PARAMS,
    )(places, *spread, left, across(left, "narrow", 1))
    low = (low + across(sent, "narrow", side).astype(F32)).astype(BF16)

    wide_cols = 2 * inner + 2 * rank_cols
    sums = pl.pallas_call(
        functools.partial(base_kernel, count, side),
        out_shape=[jax.ShapeDtypeStruct((rows, wide_cols), F32 if k == 0 else BF16) for k in range(count)],
        in_specs=[SMEM] + [VMEM] * (2 * side + 2),
        out_specs=[VMEM] * count,
        scratch_shapes=[
            pltpu.VMEM((count * rows, 2 * inner), F32),
            pltpu.VMEM((count * rows, 2 * rank_cols), BF16),
        ],
        compiler_params=PARAMS,
    )(
        places,
        mine,
        across(after(mine, sent), "narrow", 1),
        low,
        across(low, "narrow", 1),
        base_gate,
        base_up,
    )

    own = jnp.stack(
        [
            gate_right.reshape(rank_cols, inner),
            up_right.reshape(rank_cols, inner),
            jnp.swapaxes(down_left, 1, 2).reshape(rank_cols, inner),
        ]
    )
    pairs = [(g * count + z, g * count + (z ^ 2 ^ g)) for g in range(2) for z in range(count)]
    far = lax.ppermute(after(own, spread[1], spread[3], come[1]), ("groups", "wide"), pairs)
    traded = lax.ppermute(after(far, sums[0]), "groups", [(0, 1), (1, 0)])
    sums = [sums[0]] + [across(sums[k], "wide", k) for k in range(1, count)]
    near = across(own, "wide", 1)

    expert_ids = lax.broadcasted_iota(jnp.int32, (1, 1, experts), 2)
    named = routes[:, :, None] == expert_ids
    delta_ids = jnp.sum(jnp.where(named, delta_of[None, None, :], 0), axis=2)
    away = (delta_ids // held) ^ place
    away = jnp.where(away < 2, away, away ^ group)
    slots = away * held + delta_ids % held
    weight = jnp.sum(jnp.where(slots[:, :, None] == expert_ids, gate_weights[:, :, None], 0.0), axis=1)

    base, acc, hl, low = pl.pallas_call(
        functools.partial(hidden_kernel, count, held),
        out_shape=[
            jax.ShapeDtypeStruct((rows, 2 * inner), F32),
            jax.ShapeDtypeStruct((rows, inner), F32),
            jax.ShapeDtypeStruct((count, rows, rank_cols), F32),
            jax.ShapeDtypeStruct((count, rows, 2 * rank_cols), BF16),
        ],
        in_specs=[SMEM] + [VMEM] * (2 * count),
        out_specs=[VMEM] * 4,
        compiler_params=PARAMS,
    )(places, *sums, weight, own, near, far)
    hsum, kept, given = pl.pallas_call(
        functools.partial(hidden_last_kernel, count, held),
        out_shape=[
            jax.ShapeDtypeStruct((rows, inner), BF16),
            jax.ShapeDtypeStruct((rows, side * rank_cols), F32),
            jax.ShapeDtypeStruct((rows, side * rank_cols), BF16),
        ],
        in_specs=[SMEM] + [VMEM] * 6,
        out_specs=[VMEM] * 3,
        scratch_shapes=[pltpu.VMEM((count, rows, rank_cols), F32)],
        compiler_params=PARAMS,
    )(places, base, acc, hl, low, weight, traded)

    part = (kept + across(given, "narrow", 1).astype(F32)).astype(BF16)
    part = jnp.split(part, side, axis=1)
    first = swap(jnp.concatenate([hsum, part[0]], axis=1))
    low_sum = first[:, inner:].astype(F32) + sum(swap(part[b], side * b).astype(F32) for b in range(1, side))
    hs = jnp.concatenate([first[:, :inner], low_sum.astype(BF16)], axis=1)
    hs = jnp.concatenate([hs, across(hs, "narrow", side)], axis=0)
    outs = pl.pallas_call(
        functools.partial(down_kernel, count, side),
        out_shape=[jax.ShapeDtypeStruct((rows, features), F32 if k == 0 else BF16) for k in range(count)],
        in_specs=[SMEM] + [VMEM] * 4,
        out_specs=[VMEM] * count,
        scratch_shapes=[pltpu.VMEM((count * rows, features), F32)],
        compiler_params=PARAMS,
    )(places, hs, across(hs, "narrow", 1), base_down, down_right.reshape(rank_cols, features))
    return sum([outs[0]] + [ahead(outs[k], k).astype(F32) for k in range(1, count)]).astype(BF16)


def solution(mesh):
    shape = mesh.shape
    stationary = shape["groups"] == 2 and shape["wide"] == shape["narrow"] == shape["groups"] ** 2
    return jax.shard_map(
        stationary_shards if stationary else gathered_shards,
        mesh=mesh,
        in_specs=(
            P(("groups", "wide"), "narrow"),
            P(("groups", "wide"), None),
            P(("groups", "wide"), None),
            P(),
            P("wide", "narrow"),
            P("wide", "narrow"),
            P("wide", "narrow"),
            P("wide", "narrow", None),
            P("wide", None, "narrow"),
            P("wide", "narrow", None),
            P("wide", None, "narrow"),
            P("wide", "narrow", None),
            P("wide", None, "narrow"),
        ),
        out_specs=P(("groups", "wide"), "narrow"),
        check_vma=False,
    )
```

```python
import functools
import math

import jax
import jax.numpy as jnp
from jax import lax
from jax.experimental import pallas as pl
from jax.experimental.pallas import tpu as pltpu
from jax.sharding import PartitionSpec as P

F32 = jnp.float32
BF16 = jnp.bfloat16


def with_zero_row(rows):
    return jnp.concatenate([rows, jnp.zeros((1, rows.shape[1]), rows.dtype)], axis=0)


def rebuild(base_rows, left_rows, right_factor):
    product = jnp.einsum(
        "ecr,erf->ecf", left_rows, right_factor, preferred_element_type=jnp.float32
    )
    return (base_rows.astype(jnp.float32)[None] + product).astype(jnp.bfloat16)


def gathered_shards(
    tokens,
    routes,
    gate_weights,
    delta_of,
    base_gate,
    base_up,
    base_down,
    gate_left,
    gate_right,
    up_left,
    up_right,
    down_left,
    down_right,
):
    block_rows, top_count = routes.shape
    feature_part = tokens.shape[1]
    exp_here = gate_left.shape[0]
    wide_count = lax.axis_size("wide")
    experts = wide_count * exp_here
    capacity = max(2, block_rows * top_count * 5 // (4 * experts))
    slot_total = experts * capacity
    expert_ids = lax.broadcasted_iota(jnp.int32, (1, 1, experts), 2)
    onehot = (routes[:, :, None] == expert_ids).astype(jnp.float32)
    routed = jnp.sum(onehot, axis=1)
    row_index = lax.broadcasted_iota(jnp.int32, (block_rows, block_rows), 0)
    col_index = lax.broadcasted_iota(jnp.int32, (block_rows, block_rows), 1)
    earlier_mask = (col_index < row_index).astype(jnp.float32)
    before = jnp.dot(
        earlier_mask, routed, preferred_element_type=jnp.float32, precision=lax.Precision.HIGHEST
    )
    place_in = jnp.sum(onehot * before[:, None, :], axis=2).astype(jnp.int32)
    delta_ids = jnp.sum(onehot * delta_of.astype(jnp.float32)[None, None, :], axis=2).astype(
        jnp.int32
    )
    position = delta_ids * capacity + place_in
    every_row = lax.all_gather(tokens, "wide", axis=0, tiled=True)
    every_place = lax.all_gather(position, "wide", axis=0, tiled=True)
    own_first = lax.axis_index("wide") * (exp_here * capacity)
    local_place = every_place - own_first
    owned = (local_place >= 0) & (local_place < exp_here * capacity)
    block_ids = lax.broadcasted_iota(jnp.int32, every_place.shape, 0) // block_rows
    target = jnp.where(owned, block_ids * (exp_here * capacity) + local_place, slot_total)
    every_token = lax.broadcasted_iota(jnp.int32, every_place.shape, 0)
    picked_rows = (
        jnp.full((slot_total,), every_row.shape[0], jnp.int32)
        .at[target.reshape(-1)]
        .set(every_token.reshape(-1), mode="drop")
    )
    local_rows = jnp.take(with_zero_row(every_row), picked_rows, axis=0).reshape(
        wide_count, exp_here, capacity, feature_part
    )
    slot_rows = lax.all_gather(local_rows, "narrow", axis=3, tiled=True)
    left_gate, left_up, left_down = (
        lax.all_gather(gate_left, "narrow", axis=1, tiled=True),
        lax.all_gather(up_left, "narrow", axis=1, tiled=True),
        lax.all_gather(down_left, "narrow", axis=1, tiled=True),
    )
    base_rows_gate = lax.all_gather(base_gate, "wide", axis=0, tiled=True)
    base_rows_up = lax.all_gather(base_up, "wide", axis=0, tiled=True)
    columns = slot_rows
    dense_gate = rebuild(base_rows_gate, left_gate, gate_right)
    dense_up = rebuild(base_rows_up, left_up, up_right)
    gate_sum = jnp.einsum("secd,edf->secf", columns, dense_gate, preferred_element_type=jnp.float32)
    up_sum = jnp.einsum("secd,edf->secf", columns, dense_up, preferred_element_type=jnp.float32)
    hidden = (jax.nn.silu(gate_sum) * up_sum).astype(jnp.bfloat16)
    hidden_all = lax.all_gather(hidden, "narrow", axis=3, tiled=True)
    dense_down = rebuild(
        lax.all_gather(base_down, "wide", axis=0, tiled=True), left_down, down_right
    )
    columns = hidden_all
    expert_out = jnp.einsum(
        "secf,efd->secd", columns, dense_down, preferred_element_type=jnp.float32
    ).astype(jnp.bfloat16)
    returned = lax.all_to_all(expert_out, "wide", split_axis=0, concat_axis=0, tiled=True).reshape(
        slot_total, feature_part
    )
    picked = jnp.take(returned, position.reshape(-1), axis=0).reshape(
        block_rows, top_count, feature_part
    )
    mixed_out = jnp.sum(gate_weights[:, :, None] * picked.astype(jnp.float32), axis=1)
    return mixed_out.astype(jnp.bfloat16)


def dot_rows(a, b):
    return lax.dot_general(a, b, (((1,), (1,)), ((), ())), preferred_element_type=F32)


def left_kernel(count, side, place, *refs):
    xs, ls, (out, sent, held) = refs[:count], refs[count : count + side], refs[count + side :]
    rows = xs[0].shape[0]
    for m in range(count):
        held[m] = xs[m][...]
    total = jnp.zeros(out.shape, F32)
    for e in range(side):
        spots = [place[0] ^ (side * u + (lax.rem(place[1], side) ^ e)) for u in range(side)]
        total += dot_rows(jnp.concatenate([held[m] for m in spots], axis=0), ls[e][...])
    out[...] = total
    sent[...] = total.astype(BF16)


def base_kernel(count, side, place, *refs):
    xs, lows, (wg, wu), refs = refs[:side], refs[side : 2 * side], refs[2 * side : 2 * side + 2], refs[2 * side + 2 :]
    outs, (total, low) = refs[:-2], refs[-2:]
    cols = wg.shape[1]
    rows = outs[0].shape[0]
    x = jnp.concatenate([x[...] for x in xs], axis=0)
    total[:, :cols] = jnp.dot(x, wg[...], preferred_element_type=F32)
    total[:, cols:] = jnp.dot(x, wu[...], preferred_element_type=F32)
    low[...] = jnp.concatenate([low[...] for low in lows], axis=0)
    for k in range(count):
        turn = lax.rem(place[0] ^ place[1] ^ k, side)
        start = pl.multiple_of((turn * side + k // side) * rows, rows)
        outs[k][:, : 2 * cols] = total[pl.ds(start, rows), :].astype(outs[k].dtype)
        start = pl.multiple_of((turn * side + ((place[0] ^ k) // side)) * rows, rows)
        outs[k][:, 2 * cols :] = low[pl.ds(start, rows), :].astype(outs[k].dtype)


def expert_terms(k, spot, held, place, gate, up, low, weight, factors):
    rows, cols = gate.shape
    rank_cols = factors.shape[1]
    owner = lax.broadcasted_iota(jnp.int32, (rows, rank_cols), 1) // (rank_cols // held)
    here = low[k]
    sides = []
    for half in (here[:, :rank_cols], here[:, rank_cols:]):
        zero = jnp.zeros_like(half)
        sides.append(jnp.concatenate([jnp.where(owner == i, half, zero) for i in range(held)], axis=0))
    g = jnp.dot(sides[0], factors[0], preferred_element_type=F32)
    u = jnp.dot(sides[1], factors[1], preferred_element_type=F32)
    total, parts = jnp.zeros((rows, cols), F32), []
    for i in range(held):
        gi = gate + g[i * rows : (i + 1) * rows]
        ui = up + u[i * rows : (i + 1) * rows]
        h = (gi / (1.0 + jnp.exp(-gi))) * ui
        slot = spot * held + i
        hw = h * weight[:, slot : slot + 1]
        total += hw
        parts.append(hw.astype(BF16))
    back = dot_rows(jnp.concatenate(parts, axis=0), factors[2])
    block = jnp.zeros((rows, rank_cols), F32)
    for i in range(held):
        block += jnp.where(owner == i, back[i * rows : (i + 1) * rows], 0.0)
    return total, block


def hidden_kernel(count, held, place, *refs):
    gs, weight, rs = refs[:count], refs[count], refs[count + 1 : 2 * count]
    base, acc, hl, low = refs[2 * count :]
    cols = base.shape[1] // 2
    base[...] = sum(g[:, : 2 * cols].astype(F32) for g in gs)
    for k, g in enumerate(gs):
        low[k] = g[:, 2 * cols :].astype(BF16)
    total = jnp.zeros(acc.shape, F32)
    for spot, r in enumerate(rs):
        k = spot ^ place[2] if spot == count // 2 else spot
        more, hl[place[0] ^ place[1] ^ k] = expert_terms(
            k, spot, held, place, base[:, :cols], base[:, cols:], low, weight, r
        )
        total += more
    acc[...] = total


def hidden_last_kernel(count, held, place, base, acc, come, low, weight, r, hsum, *refs):
    outs, hl = refs[:-1], refs[-1]
    side = len(outs)
    cols = base.shape[1] // 2
    rank_cols = r.shape[1]
    hl[...] = come[...]
    k = (count - 1) ^ place[2]
    more, hl[place[0] ^ place[1] ^ k] = expert_terms(
        k, count - 1, held, place, base[:, :cols], base[:, cols:], low, weight, r
    )
    hsum[...] = (acc[...] + more).astype(BF16)
    for e in range(side):
        for b in range(side):
            outs[e][:, b * rank_cols : (b + 1) * rank_cols] = hl[side * b + e].astype(outs[e].dtype)


def down_kernel(count, side, place, *refs):
    blocks, (w, rd), outs, total = refs[:count], refs[count : count + 2], refs[count + 2 : -1], refs[-1]
    rows = outs[0].shape[0]
    inner = w.shape[0]
    hs = jnp.concatenate([b[...] for b in blocks], axis=0)
    total[...] = jnp.dot(hs[:, :inner], w[...], preferred_element_type=F32)
    total[...] += jnp.dot(hs[:, inner:], rd[...], preferred_element_type=F32)
    for k in range(count):
        away = lax.rem(place[0] + k, count) ^ place[1]
        start = pl.multiple_of((lax.rem(away, side) * side + away // side) * rows, rows)
        outs[k][...] = total[pl.ds(start, rows), :].astype(outs[k].dtype)


VMEM = pl.BlockSpec(memory_space=pltpu.VMEM)
SMEM = pl.BlockSpec(memory_space=pltpu.SMEM)
PARAMS = pltpu.CompilerParams(vmem_limit_bytes=24 * 2**20)


def after(a, *others):
    return lax.optimization_barrier((a, others))[0]


def stationary_shards(
    tokens,
    routes,
    gate_weights,
    delta_of,
    base_gate,
    base_up,
    base_down,
    gate_left,
    gate_right,
    up_left,
    up_right,
    down_left,
    down_right,
):
    count = lax.axis_size("wide")
    side = math.isqrt(count)
    rows = tokens.shape[0]
    held, rank = gate_left.shape[0], gate_left.shape[2]
    experts = held * count
    rank_cols = held * rank
    inner = base_gate.shape[1]
    features = base_down.shape[1]
    place, spot, group = (lax.axis_index(a) for a in ("wide", "narrow", "groups"))
    places = jnp.stack([place, spot, group]).astype(jnp.int32)

    def swap(a, k=0):
        pairs = [(i * count + j, (j ^ k) * count + i) for i in range(count) for j in range(count)]
        return lax.ppermute(a, ("wide", "narrow"), pairs)

    def across(a, axis, k):
        return lax.ppermute(a, axis, [(i, i ^ k) for i in range(count)])

    def ahead(a, k):
        return lax.ppermute(a, "wide", [(i, (i + k) % count) for i in range(count)])

    spread = []
    for m in range(count):
        pairs = [
            (w * count + j, (m ^ (w // side * side + j % side)) * count + j // side * side + w % side)
            for w in range(count)
            for j in range(count)
        ]
        spread.append(lax.ppermute(tokens, ("wide", "narrow"), pairs))

    pairs = [
        (z * count + n, z * count + (n ^ side))
        for z in range(count)
        for n in range(count)
        if z // side == n // side
    ]
    come = [lax.ppermute(spread[side * a], ("wide", "narrow"), pairs) for a in range(side)]
    holds = spot // side == place // side
    mine = jnp.concatenate([jnp.where(holds, spread[side * a], come[a]) for a in range(side)], axis=0)

    left = jnp.concatenate(
        [jnp.swapaxes(a, 1, 2).reshape(rank_cols, a.shape[1]) for a in (gate_left, up_left)], axis=0
    )
    low, sent = pl.pallas_call(
        functools.partial(left_kernel, count, side),
        out_shape=[jax.ShapeDtypeStruct((side * rows, 2 * rank_cols), kind) for kind in (F32, BF16)],
        in_specs=[SMEM] + [VMEM] * (count + side),
        out_specs=[VMEM] * 2,
        scratch_shapes=[pltpu.VMEM((count, *tokens.shape), BF16)],
        compiler_params=PARAMS,
    )(places, *spread, left, across(left, "narrow", 1))
    low = (low + across(sent, "narrow", side).astype(F32)).astype(BF16)

    wide_cols = 2 * inner + 2 * rank_cols
    sums = pl.pallas_call(
        functools.partial(base_kernel, count, side),
        out_shape=[jax.ShapeDtypeStruct((rows, wide_cols), F32 if k == 0 else BF16) for k in range(count)],
        in_specs=[SMEM] + [VMEM] * (2 * side + 2),
        out_specs=[VMEM] * count,
        scratch_shapes=[
            pltpu.VMEM((count * rows, 2 * inner), F32),
            pltpu.VMEM((count * rows, 2 * rank_cols), BF16),
        ],
        compiler_params=PARAMS,
    )(
        places,
        mine,
        across(after(mine, sent), "narrow", 1),
        low,
        across(low, "narrow", 1),
        base_gate,
        base_up,
    )

    own = jnp.stack(
        [
            gate_right.reshape(rank_cols, inner),
            up_right.reshape(rank_cols, inner),
            jnp.swapaxes(down_left, 1, 2).reshape(rank_cols, inner),
        ]
    )
    pairs = [(g * count + z, g * count + (z ^ 2 ^ g)) for g in range(2) for z in range(count)]
    far = lax.ppermute(after(own, spread[1], spread[3], come[1]), ("groups", "wide"), pairs)
    traded = lax.ppermute(after(far, sums[0]), "groups", [(0, 1), (1, 0)])
    sums = [sums[0]] + [across(sums[k], "wide", k) for k in range(1, count)]
    near = across(own, "wide", 1)

    expert_ids = lax.broadcasted_iota(jnp.int32, (1, 1, experts), 2)
    named = routes[:, :, None] == expert_ids
    delta_ids = jnp.sum(jnp.where(named, delta_of[None, None, :], 0), axis=2)
    away = (delta_ids // held) ^ place
    away = jnp.where(away < 2, away, away ^ group)
    slots = away * held + delta_ids % held
    weight = jnp.sum(jnp.where(slots[:, :, None] == expert_ids, gate_weights[:, :, None], 0.0), axis=1)

    base, acc, hl, low = pl.pallas_call(
        functools.partial(hidden_kernel, count, held),
        out_shape=[
            jax.ShapeDtypeStruct((rows, 2 * inner), F32),
            jax.ShapeDtypeStruct((rows, inner), F32),
            jax.ShapeDtypeStruct((count, rows, rank_cols), F32),
            jax.ShapeDtypeStruct((count, rows, 2 * rank_cols), BF16),
        ],
        in_specs=[SMEM] + [VMEM] * (2 * count),
        out_specs=[VMEM] * 4,
        compiler_params=PARAMS,
    )(places, *sums, weight, own, near, far)
    hsum, kept, given = pl.pallas_call(
        functools.partial(hidden_last_kernel, count, held),
        out_shape=[
            jax.ShapeDtypeStruct((rows, inner), BF16),
            jax.ShapeDtypeStruct((rows, side * rank_cols), F32),
            jax.ShapeDtypeStruct((rows, side * rank_cols), BF16),
        ],
        in_specs=[SMEM] + [VMEM] * 6,
        out_specs=[VMEM] * 3,
        scratch_shapes=[pltpu.VMEM((count, rows, rank_cols), F32)],
        compiler_params=PARAMS,
    )(places, base, acc, hl, low, weight, traded)

    part = (kept + across(given, "narrow", 1).astype(F32)).astype(BF16)
    part = jnp.split(part, side, axis=1)
    first = swap(jnp.concatenate([hsum, part[0]], axis=1))
    low_sum = first[:, inner:].astype(F32) + sum(swap(part[b], side * b).astype(F32) for b in range(1, side))
    hs = jnp.concatenate([first[:, :inner], low_sum.astype(BF16)], axis=1)
    hs = [hs, across(hs, "narrow", side)]
    hs = hs + [across(h, "narrow", 1) for h in hs]
    outs = pl.pallas_call(
        functools.partial(down_kernel, count, side),
        out_shape=[jax.ShapeDtypeStruct((rows, features), F32 if k == 0 else BF16) for k in range(count)],
        in_specs=[SMEM] + [VMEM] * (count + 2),
        out_specs=[VMEM] * count,
        scratch_shapes=[pltpu.VMEM((count * rows, features), F32)],
        compiler_params=PARAMS,
    )(places, *hs, base_down, down_right.reshape(rank_cols, features))
    return sum([outs[0]] + [ahead(outs[k], k).astype(F32) for k in range(1, count)]).astype(BF16)


def solution(mesh):
    shape = mesh.shape
    stationary = shape["groups"] == 2 and shape["wide"] == shape["narrow"] == shape["groups"] ** 2
    return jax.shard_map(
        stationary_shards if stationary else gathered_shards,
        mesh=mesh,
        in_specs=(
            P(("groups", "wide"), "narrow"),
            P(("groups", "wide"), None),
            P(("groups", "wide"), None),
            P(),
            P("wide", "narrow"),
            P("wide", "narrow"),
            P("wide", "narrow"),
            P("wide", "narrow", None),
            P("wide", None, "narrow"),
            P("wide", "narrow", None),
            P("wide", None, "narrow"),
            P("wide", "narrow", None),
            P("wide", None, "narrow"),
        ),
        out_specs=P(("groups", "wide"), "narrow"),
        check_vma=False,
    )
```
